32 devices in a mesh: layer: 2 (over x), row: 4 (over y, core), col: 4 (over z).
Axes of the slice: x: 2, y: 2, z: 4, core: 2. Of those that a mesh axis runs over, the one named last changes fastest.
Arguments:
- reflect_fwd: float32 [2, 1024, 1024], P('layer', 'row', 'col'), may hold values from -1 to 1
- transmit_fwd: float32 [2, 1024, 1024], P('layer', 'row', 'col'), may hold values from -1 to 1
- reflect_bwd: float32 [2, 1024, 1024], P('layer', 'row', 'col'), may hold values from -1 to 1
- transmit_bwd: float32 [2, 1024, 1024], P('layer', 'row', 'col'), may hold values from -1 to 1
- material_ids: int32 [2], P('layer'), may hold values from 0 to 7
- interface_gain: float32 [8, 1024], replicated, may hold values from 0.5 to 1
Outputs:
- reflect_out: float32 [2, 1024, 1024], P('layer', 'row', 'col')
- transmit_out: float32 [2, 1024, 1024], P('layer', 'row', 'col')
The draws below stay inside these ranges and needn't reach their ends.
All inputs are finite; a program needn't handle non-finite values.
Results may differ from the reference program's by a relative error of at most 0.00015.
Values sent between devices are 32-bit elements; how exact they have to be, the bound alone decides.
No kernel may reach another device: no remote copies, remote signals or barrier semaphores. Data moves between devices by JAX's collectives and lax.ppermute only.
A program may use at most 64 MiB of HBM per device.

```python
import math
import jax
import jax.numpy as jnp
from jax import lax

NTERMS = 6
NMAT = 8
M = 1024
NCOMP = 2
N_LAYER = 2


def operator_draw(key, low_diag, high_diag, spread):
    noise_key, diag_key = jax.random.split(key)
    shape_full = (N_LAYER, M, M)
    diagonal_mask = (lax.broadcasted_iota(jnp.int32, shape_full, 1) == lax.broadcasted_iota(jnp.int32, shape_full, 2)).astype(jnp.float32)
    noise = jax.random.normal(noise_key, shape_full, jnp.float32) * (spread / math.sqrt(M))
    diag_values = jax.random.uniform(diag_key, (N_LAYER, M, 1), jnp.float32, low_diag, high_diag)
    noise = jnp.clip(noise, -0.2, 0.2)
    return noise * (1.0 - diagonal_mask) + diagonal_mask * diag_values


def draw_reflect_fwd(key, part):
    return operator_draw(jax.random.fold_in(key, 11), 0.5, 0.8, 0.15)


def draw_transmit_fwd(key, part):
    return operator_draw(jax.random.fold_in(key, 23), 0.3, 0.6, 0.12)


def draw_reflect_bwd(key, part):
    return operator_draw(jax.random.fold_in(key, 37), 0.5, 0.8, 0.15)


def draw_transmit_bwd(key, part):
    return operator_draw(jax.random.fold_in(key, 41), 0.3, 0.6, 0.12)


def setup_inputs(seed: int = 0) -> dict:
    splits = jax.random.split(jax.random.key(seed), 7)
    reflect_fwd = draw_reflect_fwd(jax.random.fold_in(splits[6], 71), 0)
    transmit_fwd = draw_transmit_fwd(jax.random.fold_in(splits[6], 71), 0)
    reflect_bwd = draw_reflect_bwd(jax.random.fold_in(splits[6], 71), 0)
    transmit_bwd = draw_transmit_bwd(jax.random.fold_in(splits[6], 71), 0)
    material_ids = jax.random.randint(splits[4], (NCOMP,), 0, NMAT).astype(jnp.int32)
    interface_gain = jnp.clip(jax.random.uniform(splits[5], (NMAT, M), jnp.float32, 0.5, 1.0), 0.5, 1.0)
    return {"reflect_fwd": reflect_fwd, "transmit_fwd": transmit_fwd, "reflect_bwd": reflect_bwd, "transmit_bwd": transmit_bwd, "material_ids": material_ids, "interface_gain": interface_gain}


def product(left, right):
    return jnp.dot(left, right, precision=lax.Precision.HIGHEST)


def pair_product(reflect_a, transmit_a, reflect_back_a, transmit_back_a, reflect_b, transmit_b, weight):
    scaled_fwd = weight[:, None] * transmit_a
    scaled_bwd = transmit_back_a * weight[None, :]
    power_term = product(reflect_back_a, reflect_b)
    side_term = product(scaled_bwd, reflect_b)
    identity = jnp.eye(M, dtype=reflect_a.dtype)
    series = identity + power_term
    for repeat in range(NTERMS - 2):
        series = identity + product(power_term, series)
    middle = product(series, scaled_fwd)
    return reflect_a + product(side_term, middle), product(transmit_b, middle)


def reference(reflect_fwd, transmit_fwd, reflect_bwd, transmit_bwd, material_ids, interface_gain):
    distance = N_LAYER // 2
    gain_rows = interface_gain[material_ids]
    weights = gain_rows[:distance] * gain_rows[distance:]

    def single(operands):
        return pair_product(*operands)

    reflect_pair, transmit_pair = lax.map(single, (reflect_fwd[:distance], transmit_fwd[:distance], reflect_bwd[:distance], transmit_bwd[:distance], reflect_fwd[distance:], transmit_fwd[distance:], weights))
    reflect_out = jnp.concatenate([reflect_pair, reflect_pair], axis=0)
    transmit_out = jnp.concatenate([transmit_pair, transmit_pair], axis=0)
    return (reflect_out, transmit_out)
```

```python
import functools

import jax
import jax.numpy as jnp
from jax import lax
from jax.experimental import pallas as pl
from jax.experimental.pallas import tpu as pltpu
from jax.sharding import PartitionSpec as P

NTERMS = 6
VMEM_LIMIT = 48 * 2**20


def split(value):
    high = value.astype(jnp.bfloat16)
    return high, (value - high.astype(jnp.float32)).astype(jnp.bfloat16)


def dot(left, right):
    return jnp.dot(left, right, preferred_element_type=jnp.float32)


def dot3(left_high, left_low, right_high, right_low):
    return dot(left_high, right_high) + (dot(left_high, right_low) + dot(left_low, right_high))


def span(index, size):
    return pl.ds(pl.multiple_of(index * size, size), size)


def step_kernel(step, n_pieces, pos, *refs):
    pieces = refs[:n_pieces]
    refs = refs[n_pieces:]
    highs, lows, sums = refs[:step], refs[step : 2 * step], refs[2 * step : 3 * step]
    high, low = refs[3 * step], refs[3 * step + 1]
    out_sums = refs[3 * step + 2 :]
    rows, cols = pieces[0].shape
    for i, piece in enumerate(pieces):
        side, row = pos[2 * i], pos[2 * i + 1]
        high[side, span(row, rows), :], low[side, span(row, rows), :] = split(piece[...])
    place = pos[2 * n_pieces + step]
    for n in range(step):
        out_sums[n][...] = sums[n][...] + dot3(
            high[0], low[0], highs[n][1, span(place, cols), :], lows[n][1, span(place, cols), :]
        )
    total = dot3(high[0], low[0], high[1, span(place, cols), :], low[1, span(place, cols), :])
    for n in range(step):
        k = pos[2 * n_pieces + n]
        total += dot3(highs[n][0], lows[n][0], high[1, span(k, cols), :], low[1, span(k, cols), :])
    out_sums[step][...] = total


def last_kernel(blocks, row_pieces, pos, *refs):
    highs, lows, sums = refs[:blocks], refs[blocks : 2 * blocks], refs[2 * blocks : 3 * blocks]
    left = refs[3 * blocks : 4 * blocks]
    refs = refs[4 * blocks :]
    panels = refs[:row_pieces]
    weight, reflect, out, power_high, power_low, left_high, left_low, base, state, z_high, z_low = refs[row_pieces:]
    rows, cols = left[0].shape
    upper = pos[0] == 0
    for i, panel in enumerate(panels):
        base[span(pos[1 + i], rows), :] = panel[...]
    places = [pos[1 + row_pieces + j] for j in range(blocks)]

    def take(source):
        for j in range(blocks):
            here = pl.ds(j * cols, cols)
            z_high[here, :], z_low[here, :] = split(source[span(places[j], cols), :])

    for j in range(blocks):
        here = pl.ds(j * cols, cols)
        power_high[:, here], power_low[:, here] = split(sums[j][...])

    @pl.when(upper)
    def _():
        for n in range(blocks):
            total = None
            for j in range(blocks):
                scaled = left[j][...] * weight[pl.ds(places[j], 1), :]
                term = dot3(*split(scaled), highs[n][1, span(places[j], cols), :], lows[n][1, span(places[j], cols), :])
                total = term if total is None else total + term
            here = pl.ds(n * cols, cols)
            left_high[:, here], left_low[:, here] = split(total)

    @pl.when(jnp.logical_not(upper))
    def _():
        for n in range(blocks):
            here = pl.ds(n * cols, cols)
            left_high[:, here], left_low[:, here] = split(left[n][...])

    take(base)

    @pl.loop(0, NTERMS - 1)
    def _(_):
        state[...] = base[...] + dot3(power_high[...], power_low[...], z_high[...], z_low[...])
        take(state)

    result = dot3(left_high[...], left_low[...], z_high[...], z_low[...])

    @pl.when(upper)
    def _():
        out[...] = reflect[...] + result

    @pl.when(jnp.logical_not(upper))
    def _():
        out[...] = result


def vmem(count):
    return [pl.BlockSpec(memory_space=pltpu.VMEM)] * count


def call(kernel, pos, operands, outs, scratch, aliases, flops):
    moved = sum(a.size * a.dtype.itemsize for a in operands)
    return pl.pallas_call(
        kernel,
        out_shape=outs,
        in_specs=[pl.BlockSpec(memory_space=pltpu.SMEM)] + vmem(len(operands)),
        out_specs=jax.tree.map(lambda _: vmem(1)[0], outs),
        scratch_shapes=scratch,
        input_output_aliases=aliases,
        compiler_params=pltpu.CompilerParams(vmem_limit_bytes=VMEM_LIMIT),
        cost_estimate=pl.CostEstimate(flops=flops, bytes_accessed=moved, transcendentals=0),
    )(pos, *operands)


def on_device(reflect_fwd, transmit_fwd, reflect_bwd, transmit_bwd, material_ids, interface_gain):
    reflect_fwd, transmit_fwd, reflect_bwd, transmit_bwd = (
        a[0] for a in (reflect_fwd, transmit_fwd, reflect_bwd, transmit_bwd)
    )
    rows, cols = reflect_fwd.shape
    layers, row_count, blocks = (lax.axis_size(a) for a in ("layer", "row", "col"))
    order = rows * row_count
    distance = layers // 2
    cores = 2 if row_count % 2 == 0 else 1
    chips = row_count // cores
    layer, row, col = (lax.axis_index(a) for a in ("layer", "row", "col"))
    upper = layer < distance
    side, chip, core = jnp.where(upper, 0, 1), row // cores, row % cores

    def plane(value, even, odd):
        route = []
        for here in range(layers):
            for there in range(row_count):
                flip, hop = (even, odd)[there % cores]
                target = (here + distance) % layers if flip else here
                route.append((here * row_count + there, target * row_count + (there + hop * cores) % row_count))
        return lax.ppermute(value, ("layer", "row"), route)

    def sibling(value):
        return lax.ppermute(value, "row", [(i, i ^ 1) for i in range(row_count)])

    def onward(value):
        return lax.ppermute(value, "col", [(i, (i + 1) % blocks) for i in range(blocks)])

    own = jnp.where(upper, reflect_bwd, reflect_fwd)
    left_own = jnp.where(upper, transmit_bwd, transmit_fwd)
    own_gain = lax.dynamic_index_in_dim(interface_gain, material_ids[0], 0, keepdims=False)
    extended = jnp.concatenate([transmit_fwd, own_gain.reshape(-1, cols)], axis=0)
    across = plane(extended, (1, 0), (1, 0))
    weight = own_gain * across[rows:].reshape(-1)
    row_gain = lax.dynamic_slice_in_dim(weight, row * rows, rows)
    panel = row_gain[:, None] * jnp.where(upper, transmit_fwd, across[:rows])

    hops = [((0, 0), (0, 0))]
    if chips == 2:
        hops += [((1, 0), (0, 1)), ((0, 1), (1, 0)), ((1, 1), (1, 1))]
    else:
        hops += [((1, 0), (1, 0))]
        hops += [((f, h), (f, h)) for f in (0, 1) for h in range(1, chips)]

    def gather(piece):
        found = [piece]
        if chips == 2:
            first = plane(piece, *hops[1])
            found += [first, plane(piece, *hops[2]), plane(first, *hops[2])]
        else:
            first = plane(piece, (1, 0), (1, 0))
            found += [first]
            found += [plane(v, (0, h), (0, h)) for v in (piece, first) for h in range(1, chips)]
        if cores == 2:
            found += [sibling(v) for v in found]
        return found

    origins = []
    for other in range(cores):
        for even, odd in hops:
            on = core if other == 0 else 1 - core
            flip = jnp.where(on == 0, even[0], odd[0])
            hop = jnp.where(on == 0, even[1], odd[1])
            origins += [jnp.where(flip == 1, 1 - side, side), (chip - hop) % chips * cores + on]
    places = [(col - j) % blocks for j in range(blocks)]
    n_pieces = cores * len(hops)
    pos = jnp.stack([jnp.asarray(v, jnp.int32) for v in origins + places])

    highs, lows, sums = [], [], []
    piece = own
    both = jax.ShapeDtypeStruct((2, order, cols), jnp.bfloat16)
    total = jax.ShapeDtypeStruct((order, cols), jnp.float32)
    for step in range(blocks):
        pieces = gather(piece)
        if step + 1 < blocks:
            piece = onward(piece)
        results = call(
            functools.partial(step_kernel, step, n_pieces),
            pos,
            pieces + highs + lows + sums,
            [both, both] + [total] * (step + 1),
            [],
            {1 + n_pieces + 2 * step + n: 2 + n for n in range(step)},
            6 * (2 * step + 1) * order * cols * cols,
        )
        highs, lows, sums = highs + [results[0]], lows + [results[1]], list(results[2:])

    left = [left_own]
    for step in range(blocks - 1):
        left.append(onward(left[-1]))

    panels, starts = [panel], [row]
    for hop in range(1, chips):
        panels.append(plane(panel, (0, hop), (0, hop)))
        starts.append((row - hop * cores) % row_count)
    if cores == 2:
        panels += [sibling(v) for v in panels]
        starts += [v ^ 1 for v in starts]

    last_pos = jnp.stack([jnp.asarray(v, jnp.int32) for v in [side] + starts + places])
    result = call(
        functools.partial(last_kernel, blocks, len(panels)),
        last_pos,
        highs + lows + sums + left + panels + [weight.reshape(-1, cols), reflect_fwd],
        jax.ShapeDtypeStruct((rows, cols), jnp.float32),
        [pltpu.VMEM((order, order), jnp.bfloat16)] * 2
        + [pltpu.VMEM((rows, order), jnp.bfloat16)] * 2
        + [pltpu.VMEM((order, cols), jnp.float32)] * 2
        + [pltpu.VMEM((order, cols), jnp.bfloat16)] * 2,
        {},
        6 * NTERMS * order * order * cols,
    )
    swapped = plane(result, (1, 0), (1, 0))
    return jnp.where(upper, result, swapped)[None], jnp.where(upper, swapped, result)[None]


def solution(mesh):
    block = P("layer", "row", "col")
    return jax.shard_map(
        on_device,
        mesh=mesh,
        in_specs=(block, block, block, block, P("layer"), P()),
        out_specs=(block, block),
        check_vma=False,
    )
```

```python
import functools

import jax
import jax.numpy as jnp
from jax import lax
from jax.experimental import pallas as pl
from jax.experimental.pallas import tpu as pltpu
from jax.sharding import PartitionSpec as P

NTERMS = 6
MIB = 2**20
TILE = 8
GATE = 10**11


class Grid:
    def __init__(self, shape, layers, row_count, blocks):
        self.shape = shape
        self.layers, self.row_count, self.blocks = layers, row_count, blocks
        self.distance = layers // 2
        self.cores = 2 if row_count % 2 == 0 else 1
        self.chips = row_count // self.cores
        self.hops = [((0, 0), (0, 0))]
        if self.chips == 2:
            self.hops += [((1, 0), (0, 1)), ((0, 1), (1, 0)), ((1, 1), (1, 1))]
        else:
            self.hops += [((1, 0), (1, 0))]
            self.hops += [((f, h), (f, h)) for f in (0, 1) for h in range(1, self.chips)]

    def upper(self):
        return lax.axis_index("layer") < self.distance

    def row(self):
        return lax.axis_index("row")

    def place(self, k):
        hop = k // 2 if k % 2 == 0 else self.blocks - k // 2 - 1
        return lax.rem(lax.axis_index("col") + hop, self.blocks)

    def row_of(self, hop, other):
        row = self.row()
        core = lax.rem(row, self.cores)
        chip = lax.rem(lax.div(row, self.cores) + self.chips - hop, self.chips)
        return chip * self.cores + (self.cores - 1 - core if other else core)

    def origins(self):
        side = jnp.where(self.upper(), 0, 1)
        odd = lax.rem(self.row(), self.cores)
        found = []
        for other in range(self.cores):
            for even_hop, odd_hop in self.hops:
                on_odd = (1 - odd if other else odd) == 1
                flip = jnp.where(on_odd, odd_hop[0], even_hop[0])
                hop = jnp.where(on_odd, odd_hop[1], even_hop[1])
                found.append((jnp.where(flip == 1, 1 - side, side), self.row_of(hop, other)))
        return found


def split(value):
    high = value.astype(jnp.bfloat16)
    return high, (value - high.astype(jnp.float32)).astype(jnp.bfloat16)


def dot(left, right):
    return jnp.dot(left, right, preferred_element_type=jnp.float32)


def dot3(left_high, left_low, right_high, right_low):
    return dot(left_high, right_high) + (dot(left_high, right_low) + dot(left_low, right_high))


def span(index, size):
    return pl.ds(pl.multiple_of(index * size, size), size)


def fetch(grid, first, second, out, sem):
    @pl.when(grid.upper())
    def _():
        pltpu.make_async_copy(first.at[0], out, sem).start()

    @pl.when(jnp.logical_not(grid.upper()))
    def _():
        pltpu.make_async_copy(second.at[0], out, sem).start()

    return pltpu.make_async_copy(first.at[0], out, sem)


def choose_kernel(grid, first, second, *refs):
    out, sem = refs[-2:]
    fetch(grid, first, second, out, sem).wait()


def panel_kernel(grid, start, gains, *refs):
    rows, cols = grid.shape
    panel, weight = refs[-2:]
    height = start + rows + TILE
    pieces = [ref.at[pl.ds(i, height), :] for ref in refs[:-2] for i in range(0, ref.shape[0], height)]
    for piece, (side, row) in zip(pieces, grid.origins()):
        @pl.when(side == 0)
        def _(piece=piece, row=row):
            panel[span(row, rows), :] = piece[start : start + rows, :]

    def gain(piece, i):
        number = piece[start + rows : start + rows + 1, :]
        here = pl.ds(i * cols, cols)
        return sum(jnp.where(number == m, gains[m : m + 1, here], 0.0) for m in range(gains.shape[0]))

    for i in range(gains.shape[1] // cols):
        weight[i : i + 1, :] = gain(pieces[0], i) * gain(pieces[len(grid.hops) - 1], i)
    for row in range(grid.row_count):
        here = weight[row * rows // cols : row * rows // cols + 1, :]
        column = jnp.concatenate([here] * 8, axis=0).T[:, :1]
        panel[row * rows : (row + 1) * rows, :] = panel[row * rows : (row + 1) * rows, :] * column


def gate_kernel(count, *refs):
    for value, out in zip(refs[:count], refs[-count:]):
        out[...] = value[...]


def unpack_kernel(whole, *outs):
    rows = outs[0].shape[0]
    for i, out in enumerate(outs):
        out[...] = whole[i * rows : (i + 1) * rows, :]


def pack_kernel(parts, *refs):
    here = 0
    for ref, (start, stop) in zip(refs, parts):
        refs[-1][here : here + stop - start, :] = ref[start:stop, :]
        here += stop - start


def absorb_kernel(grid, done, new, height, *refs):
    rows, cols = grid.shape
    n_pieces = grid.cores * len(grid.hops)
    pieces = []
    while len(pieces) < n_pieces:
        pieces += [refs[0].at[pl.ds(i, height), :] for i in range(0, refs[0].shape[0], height)]
        refs = refs[1:]
    old, sums, refs = refs[: 2 * done], refs[2 * done : 3 * done], refs[3 * done :]
    refs = refs[-(3 * new + done) :]
    fresh, out_sums = refs[: 2 * new], refs[2 * new :]
    highs, lows = old[:done] + fresh[:new], old[done:] + fresh[new:]
    for piece, (side, row) in zip(pieces, grid.origins()):
        for j in range(new):
            high, low = split(piece[j * rows : (j + 1) * rows, :])
            highs[done + j][side, span(row, rows), :] = high
            lows[done + j][side, span(row, rows), :] = low
    for n in range(done + new):
        total = sums[n][...] if n < done else None
        for k in range(done if n < done else 0, done + new):
            here = span(grid.place(k), cols)
            term = dot3(highs[k][0], lows[k][0], highs[n][1, here, :], lows[n][1, here, :])
            total = term if total is None else total + term
        out_sums[n][...] = total


def last_kernel(grid, *refs):
    blocks = grid.blocks
    highs, lows, sums = refs[:blocks], refs[blocks : 2 * blocks], refs[2 * blocks : 3 * blocks]
    left, refs = refs[3 * blocks : 4 * blocks], refs[4 * blocks :]
    base, weight, reflect, out, power_high, power_low, left_high, left_low, state, z_high, z_low = refs
    rows, cols = left[0].shape
    upper = grid.upper()
    places = [grid.place(j) for j in range(blocks)]

    def take(source):
        for j in range(blocks):
            here = pl.ds(j * cols, cols)
            z_high[here, :], z_low[here, :] = split(source[span(places[j], cols), :])

    for j in range(blocks):
        here = pl.ds(j * cols, cols)
        power_high[:, here], power_low[:, here] = split(sums[j][...])

    @pl.when(upper)
    def _():
        for n in range(blocks):
            total = None
            for j in range(blocks):
                scaled = left[j][...] * weight[pl.ds(places[j], 1), :]
                term = dot3(*split(scaled), highs[n][1, span(places[j], cols), :], lows[n][1, span(places[j], cols), :])
                total = term if total is None else total + term
            here = pl.ds(n * cols, cols)
            left_high[:, here], left_low[:, here] = split(total)

    @pl.when(jnp.logical_not(upper))
    def _():
        for n in range(blocks):
            here = pl.ds(n * cols, cols)
            left_high[:, here], left_low[:, here] = split(left[n][...])

    take(base)

    @pl.loop(0, NTERMS - 1)
    def _(_):
        state[...] = base[...] + dot3(power_high[...], power_low[...], z_high[...], z_low[...])
        take(state)

    result = dot3(left_high[...], left_low[...], z_high[...], z_low[...])

    @pl.when(upper)
    def _():
        out[...] = reflect[0] + result

    @pl.when(jnp.logical_not(upper))
    def _():
        out[...] = result


def finish_kernel(grid, own, across, reflect, transmit):
    upper = grid.upper()
    reflect[0] = jnp.where(upper, own[...], across[...])
    transmit[0] = jnp.where(upper, across[...], own[...])


def call(kernel, outs, operands, scalars=(), loose=(), far=(), scratch=(), aliases=None, flops=0, limit=4 * MIB):
    spaces = [pltpu.VMEM] * len(operands)
    for numbers, space in ((scalars, pltpu.SMEM), (far, pltpu.HBM), (loose, pl.ANY)):
        for i in numbers:
            spaces[i] = space
    specs = [pl.BlockSpec(memory_space=space) for space in spaces]
    return pl.pallas_call(
        kernel,
        out_shape=outs,
        in_specs=specs,
        out_specs=jax.tree.map(lambda _: pl.BlockSpec(memory_space=pltpu.VMEM), outs),
        scratch_shapes=list(scratch),
        input_output_aliases=aliases or {},
        compiler_params=pltpu.CompilerParams(vmem_limit_bytes=limit),
        cost_estimate=pl.CostEstimate(flops=flops, bytes_accessed=0, transcendentals=0),
    )(*operands)


def single(*shape):
    return jax.ShapeDtypeStruct(shape, jnp.float32)


def gate(values, *needs):
    count = len(values)
    kernel = functools.partial(gate_kernel, count)
    return call(kernel, [single(*v.shape) for v in values], [*values, *needs], loose=range(count, count + len(needs)), flops=GATE)


def pack(blocks, *needs):
    blocks = [b if isinstance(b, tuple) else (b, 0, b.shape[0]) for b in blocks]
    parts = [b[1:] for b in blocks]
    arrays = [b[0] for b in blocks]
    shape = (sum(stop - start for start, stop in parts), arrays[0].shape[1])
    loose = range(len(arrays), len(arrays) + len(needs))
    return call(functools.partial(pack_kernel, parts), single(*shape), [*arrays, *needs], loose=loose)


def unpack(whole, count):
    rows, cols = whole.shape
    return call(unpack_kernel, [single(rows // count, cols)] * count, [whole])


def on_device(reflect_fwd, transmit_fwd, reflect_bwd, transmit_bwd, material_ids, interface_gain):
    rows, cols = reflect_fwd.shape[1:]
    grid = Grid((rows, cols), *(lax.axis_size(a) for a in ("layer", "row", "col")))
    blocks, hops, cores, chips = grid.blocks, grid.hops, grid.cores, grid.chips
    order = rows * grid.row_count

    def plane(value, hop):
        route = []
        for layer in range(grid.layers):
            for row in range(grid.row_count):
                flip, on = hop[row % cores]
                target = (layer + grid.distance) % grid.layers if flip else layer
                route.append((layer * grid.row_count + row, target * grid.row_count + (row + on * cores) % grid.row_count))
        return lax.ppermute(value, ("layer", "row"), route)

    def both_cores(hop):
        return (hop, hop)

    def sibling(value):
        return lax.ppermute(value, "row", [(i, i ^ 1) for i in range(grid.row_count)])

    def ring(found, top=None):
        k = len(found)
        source = found[max(k - 2, 0)] if top is None else top
        shift = 1 if k % 2 else -1
        found.append(lax.ppermute(source, "col", [(i, (i + shift) % blocks) for i in range(blocks)]))

    def choose(first, second, *late):
        return call(
            functools.partial(choose_kernel, grid),
            single(rows, cols),
            [first, second, *late],
            far=(0, 1),
            loose=range(2, 2 + len(late)),
            scratch=[pltpu.SemaphoreType.DMA],
        )

    highs, lows, sums = [], [], []
    half = jax.ShapeDtypeStruct((2, order, cols), jnp.bfloat16)

    def absorb(pieces, new, height, weight, needs):
        nonlocal highs, lows, sums
        done = len(highs)
        operands = pieces + highs + lows + sums
        results = call(
            functools.partial(absorb_kernel, grid, done, new, height),
            [half] * (2 * new) + [single(order, cols)] * (done + new),
            operands + list(needs),
            loose=range(len(operands), len(operands) + len(needs)),
            aliases={len(operands) - done + n: 2 * new + n for n in range(done)},
            flops=int(weight * 6 * new * (2 * done + new) * order * cols * cols),
        )
        results = list(results)
        highs, lows, sums = highs + results[:new], lows + results[new : 2 * new], results[2 * new :]

    def along(value, shift):
        return lax.ppermute(value, "col", [(i, (i + shift) % blocks) for i in range(blocks)])

    def a_hop(value):
        return plane(value, hops[1])

    def b_hop(value):
        return plane(value, hops[2])

    p0 = jnp.where(grid.upper(), reflect_bwd[0], reflect_fwd[0])
    number = jnp.broadcast_to(material_ids.astype(jnp.float32), (TILE, cols))
    e0 = jnp.concatenate([p0, transmit_fwd[0], number], axis=0)

    token = number

    def step(*values):
        nonlocal token
        token, *rest = gate([token, *values])
        return rest

    p0, e0 = step(p0, e0)
    p1, a0 = along(p0, 1), a_hop(e0)
    p0, e0 = step(p0, e0)
    p2, b0 = along(p0, -1), b_hop(e0)
    p1, a0 = step(p1, a0)
    p3, a1, d0 = along(p1, 1), a_hop(p1), b_hop(a0)
    p1, p2, b0 = step(p1, p2, b0)
    b1, a2 = b_hop(p1), a_hop(p2)
    l0 = choose(transmit_bwd, transmit_fwd, p1)
    p2, p3, a1, d0, l0 = step(p2, p3, a1, d0, l0)
    d1, a3, b2 = b_hop(a1), a_hop(p3), b_hop(p2)
    b1, a2, l0 = step(b1, a2, l0)
    d2, l1 = b_hop(a2), along(l0, 1)
    d1, a3, b2, p3 = step(d1, a3, b2, p3)
    d3, b3 = b_hop(a3), b_hop(p3)
    mine01 = []
    for zero, one in ((e0, p1), (a0, a1), (b0, b1), (d0, d1)):
        mine01 += [(zero, 0, rows), one, (zero, rows, zero.shape[0])]
    mine01 = pack(mine01)
    theirs01 = sibling(mine01)
    d2, l1, l0 = step(d2, l1, l0)
    l2 = along(l0, -1)
    mine2 = pack([p2, a2, b2, d2])
    theirs2 = sibling(mine2)
    d3, b3, theirs01 = step(d3, b3, theirs01)
    l3 = along(l1, 1)
    mine3 = pack([p3, a3, b3, d3])
    theirs3 = sibling(mine3)
    absorb([mine01, theirs01], 2, 3 * rows + TILE, 1, [])
    theirs2, l2 = step(theirs2, l2)
    panel, weight = call(
        functools.partial(panel_kernel, grid, 2 * rows),
        [single(order, cols), single(-(-order // cols // TILE) * TILE, cols)],
        [interface_gain, mine01, theirs01],
    )
    absorb([mine2, theirs2], 1, rows, 1, [])
    absorb([mine3, theirs3], 1, rows, 1, [])
    left = [l0, l1, l2, l3]

    result = call(
        functools.partial(last_kernel, grid),
        single(rows, cols),
        highs + lows + sums + left + [panel, weight, reflect_fwd],
        scratch=[pltpu.VMEM((order, order), jnp.bfloat16)] * 2
        + [pltpu.VMEM((rows, order), jnp.bfloat16)] * 2
        + [pltpu.VMEM((order, cols), jnp.float32)]
        + [pltpu.VMEM((order, cols), jnp.bfloat16)] * 2,
        flops=6 * NTERMS * order * order * cols,
        limit=16 * MIB,
    )
    across = plane(result, both_cores((1, 0)))
    outs = [single(1, rows, cols)] * 2
    return tuple(call(functools.partial(finish_kernel, grid), outs, [result, across]))


def solution(mesh):
    block = P("layer", "row", "col")
    return jax.shard_map(
        on_device,
        mesh=mesh,
        in_specs=(block, block, block, block, P("layer"), P()),
        out_specs=(block, block),
        check_vma=False,
    )
```

```python
import functools

import jax
import jax.numpy as jnp
from jax import lax
from jax.experimental import pallas as pl
from jax.experimental.pallas import tpu as pltpu
from jax.sharding import PartitionSpec as P

NTERMS = 6
MIB = 2**20
TILE = 8
GATE = 2 * 10**10

SLOTS = {
    "p1": (0, 3),
    "a0": (1, 2),
    "b0": (1, 3),
    "d0": (2, 4),
    "q2": (2, 5),
    "q3": (3, 6),
    "a1": (3, 5),
    "b1": (4, 6),
    "d1": (5, 7),
    "a2": (5, 7),
    "b2": (6, 8),
    "a3": (6, 8),
    "d2": (7, 9),
    "b3": (7, 9),
    "t01": (7, 9),
    "d3": (8, 10),
    "l3": (8, 11),
    "t2": (9, 11),
    "tx": (9, 11),
    "t3": (10, 12),
}
KERNELS = {'01': 10, '2': 12}
ANCHOR = 12


class Grid:
    def __init__(self, shape, layers, row_count, blocks):
        self.shape = shape
        self.layers, self.row_count, self.blocks = layers, row_count, blocks
        self.distance = layers // 2
        self.cores = 2 if row_count % 2 == 0 else 1
        self.chips = row_count // self.cores
        self.hops = [((0, 0), (0, 0))]
        if self.chips == 2:
            self.hops += [((1, 0), (0, 1)), ((0, 1), (1, 0)), ((1, 1), (1, 1))]
        else:
            self.hops += [((1, 0), (1, 0))]
            self.hops += [((f, h), (f, h)) for f in (0, 1) for h in range(1, self.chips)]

    def upper(self):
        return lax.axis_index("layer") < self.distance

    def row(self):
        return lax.axis_index("row")

    def place(self, k):
        hop = k // 2 if k % 2 == 0 else self.blocks - k // 2 - 1
        return lax.rem(lax.axis_index("col") + hop, self.blocks)

    def row_of(self, hop, other):
        row = self.row()
        core = lax.rem(row, self.cores)
        chip = lax.rem(lax.div(row, self.cores) + self.chips - hop, self.chips)
        return chip * self.cores + (self.cores - 1 - core if other else core)

    def origins(self):
        side = jnp.where(self.upper(), 0, 1)
        odd = lax.rem(self.row(), self.cores)
        found = []
        for other in range(self.cores):
            for even_hop, odd_hop in self.hops:
                on_odd = (1 - odd if other else odd) == 1
                flip = jnp.where(on_odd, odd_hop[0], even_hop[0])
                hop = jnp.where(on_odd, odd_hop[1], even_hop[1])
                found.append((jnp.where(flip == 1, 1 - side, side), self.row_of(hop, other)))
        return found


def split(value):
    high = value.astype(jnp.bfloat16)
    return high, (value - high.astype(jnp.float32)).astype(jnp.bfloat16)


def dot(left, right):
    return jnp.dot(left, right, preferred_element_type=jnp.float32)


def dot3(left_high, left_low, right_high, right_low):
    return dot(left_high, right_high) + (dot(left_high, right_low) + dot(left_low, right_high))


def span(index, size):
    return pl.ds(pl.multiple_of(index * size, size), size)


def fetch(grid, first, second, out, sem):
    @pl.when(grid.upper())
    def _():
        pltpu.make_async_copy(first.at[0], out, sem).start()

    @pl.when(jnp.logical_not(grid.upper()))
    def _():
        pltpu.make_async_copy(second.at[0], out, sem).start()

    return pltpu.make_async_copy(first.at[0], out, sem)


def choose_kernel(grid, first, second, *refs):
    out, sem = refs[-2:]
    fetch(grid, first, second, out, sem).wait()


def number_kernel(ids, out, number, sem):
    copy = pltpu.make_async_copy(ids, number, sem)
    copy.start()
    copy.wait()
    out[...] = jnp.full(out.shape, number[0].astype(jnp.float32))


def extend_kernel(piece, block, number, out):
    rows = piece.shape[0]
    out[:rows, :] = piece[...]
    out[rows : 2 * rows, :] = block[0]
    out[2 * rows :, :] = number[...]


def panel_kernel(grid, start, gains, *refs):
    rows, cols = grid.shape
    panel, weight = refs[-2:]
    height = start + rows + TILE
    pieces = [ref.at[pl.ds(i, height), :] for ref in refs[:-2] for i in range(0, ref.shape[0], height)]
    for piece, (side, row) in zip(pieces, grid.origins()):
        @pl.when(side == 0)
        def _(piece=piece, row=row):
            panel[span(row, rows), :] = piece[start : start + rows, :]

    def gain(piece, i):
        number = piece[start + rows : start + rows + 1, :]
        here = pl.ds(i * cols, cols)
        return sum(jnp.where(number == m, gains[m : m + 1, here], 0.0) for m in range(gains.shape[0]))

    for i in range(gains.shape[1] // cols):
        weight[i : i + 1, :] = gain(pieces[0], i) * gain(pieces[len(grid.hops) - 1], i)
    for row in range(grid.row_count):
        here = weight[row * rows // cols : row * rows // cols + 1, :]
        column = jnp.concatenate([here] * 8, axis=0).T[:, :1]
        panel[row * rows : (row + 1) * rows, :] = panel[row * rows : (row + 1) * rows, :] * column


def gate_kernel(count, *refs):
    for value, out in zip(refs[:count], refs[-count:]):
        out[...] = value[...]


def unpack_kernel(whole, *outs):
    rows = outs[0].shape[0]
    for i, out in enumerate(outs):
        out[...] = whole[i * rows : (i + 1) * rows, :]


def pack_kernel(parts, *refs):
    here = 0
    for ref, (start, stop) in zip(refs, parts):
        refs[-1][here : here + stop - start, :] = ref[start:stop, :]
        here += stop - start


def ingest(grid, refs, new, height, highs, lows):
    rows = grid.shape[0]
    pieces = [ref.at[pl.ds(i, height), :] for ref in refs for i in range(0, ref.shape[0], height)]
    for piece, (side, row) in zip(pieces, grid.origins()):
        for j in range(new):
            high, low = split(piece[j * rows : (j + 1) * rows, :])
            highs[j][side, span(row, rows), :] = high
            lows[j][side, span(row, rows), :] = low


def absorb_kernel(grid, done, new, height, mine, theirs, *refs):
    cols = grid.shape[1]
    old, sums = refs[: 2 * done], refs[2 * done : 3 * done]
    refs = refs[-(3 * new + done) :]
    fresh, out_sums = refs[: 2 * new], refs[2 * new :]
    highs, lows = old[:done] + fresh[:new], old[done:] + fresh[new:]
    ingest(grid, [mine, theirs], new, height, fresh[:new], fresh[new:])
    for n in range(done + new):
        total = sums[n][...] if n < done else None
        for k in range(done if n < done else 0, done + new):
            here = span(grid.place(k), cols)
            term = dot3(highs[k][0], lows[k][0], highs[n][1, here, :], lows[n][1, here, :])
            total = term if total is None else total + term
        out_sums[n][...] = total


def horner_kernel(grid, *refs):
    rows, cols = grid.shape
    blocks = grid.blocks
    old = blocks - 1
    mine, theirs, refs = refs[0], refs[1], refs[2:]
    highs, lows, sums, refs = refs[:old], refs[old : 2 * old], refs[2 * old : 3 * old], refs[3 * old :]
    panel, _, out, high, low, power_high, power_low, pair = refs
    width = out.shape[1]
    ingest(grid, [mine, theirs], 1, rows, [high], [low])
    highs, lows = (*highs, high), (*lows, low)
    places = [grid.place(j) for j in range(blocks)]
    for n in range(blocks):
        total = sums[n][...] if n < old else None
        for k in range(old if n < old else 0, blocks):
            here = span(places[k], cols)
            term = dot3(highs[k][0], lows[k][0], highs[n][1, here, :], lows[n][1, here, :])
            total = term if total is None else total + term
        here = pl.ds(n * cols, cols)
        power_high[:, here], power_low[:, here] = split(total)

    ours = span(lax.rem(grid.row(), grid.cores), width)

    def take(read):
        for j in range(blocks):
            z_high, z_low = split(read(span(places[j], cols)))
            here = pl.ds(j * cols, cols)
            pair[here, :width], pair[here, width:] = z_high, z_low

    take(lambda here: panel[here, ours])

    @pl.loop(0, NTERMS - 1)
    def _(_):
        both = dot(power_high[...], pair[...])
        rest = dot(power_low[...], pair[:, :width])
        out[...] = panel[:, ours] + (both[:, :width] + (both[:, width:] + rest))
        take(lambda here: out[here, :])


def left_kernel(grid, *refs):
    blocks = grid.blocks
    highs, lows, left, (weight, _, left_high, left_low) = refs[:blocks], refs[blocks : 2 * blocks], refs[2 * blocks : 3 * blocks], refs[3 * blocks :]
    rows, cols = grid.shape
    places = [grid.place(j) for j in range(blocks)]
    left = [ref.at[pl.ds(ref.shape[0] - rows, rows), :] for ref in left]

    @pl.when(grid.upper())
    def _():
        scaled = [split(left[j][...] * weight[pl.ds(places[j], 1), :]) for j in range(blocks)]
        for n in range(blocks):
            total = None
            for j in range(blocks):
                term = dot3(*scaled[j], highs[n][1, span(places[j], cols), :], lows[n][1, span(places[j], cols), :])
                total = term if total is None else total + term
            here = pl.ds(n * cols, cols)
            left_high[:, here], left_low[:, here] = split(total)

    @pl.when(jnp.logical_not(grid.upper()))
    def _():
        for n in range(blocks):
            here = pl.ds(n * cols, cols)
            left_high[:, here], left_low[:, here] = split(left[n][...])


def last_kernel(grid, left_high, left_low, reflect, *refs):
    parts, (out, z_high, z_low) = refs[:-3], refs[-3:]
    cols = grid.shape[1]
    width = parts[0].shape[1]
    core = lax.rem(grid.row(), grid.cores)
    for i, part in enumerate(parts):
        ours = span(core if i == 0 else 1 - core, width)
        for j in range(grid.blocks):
            here = pl.ds(j * cols, cols)
            z_high[here, ours], z_low[here, ours] = split(part[span(grid.place(j), cols), :])
    result = dot3(left_high[...], left_low[...], z_high[...], z_low[...])
    out[...] = jnp.where(grid.upper(), reflect[0] + result, result)


def finish_kernel(grid, own, across, reflect, transmit):
    upper = grid.upper()
    reflect[0] = jnp.where(upper, own[...], across[...])
    transmit[0] = jnp.where(upper, across[...], own[...])


def call(kernel, outs, operands, scalars=(), loose=(), far=(), scratch=(), aliases=None, flops=0, moved=0, limit=4 * MIB):
    spaces = [pltpu.VMEM] * len(operands)
    for numbers, space in ((scalars, pltpu.SMEM), (far, pltpu.HBM), (loose, pl.ANY)):
        for i in numbers:
            spaces[i] = space
    specs = [pl.BlockSpec(memory_space=space) for space in spaces]
    return pl.pallas_call(
        kernel,
        out_shape=outs,
        in_specs=specs,
        out_specs=jax.tree.map(lambda _: pl.BlockSpec(memory_space=pltpu.VMEM), outs),
        scratch_shapes=list(scratch),
        input_output_aliases=aliases or {},
        compiler_params=pltpu.CompilerParams(vmem_limit_bytes=limit),
        cost_estimate=pl.CostEstimate(flops=flops, bytes_accessed=moved, transcendentals=0),
    )(*operands)


def single(*shape):
    return jax.ShapeDtypeStruct(shape, jnp.float32)


def gate(values, *needs):
    count = len(values)
    kernel = functools.partial(gate_kernel, count)
    return call(kernel, [single(*v.shape) for v in values], [*values, *needs], loose=range(count, count + len(needs)), flops=GATE, moved=10 * GATE)


def pack(blocks, *needs):
    blocks = [b if isinstance(b, tuple) else (b, 0, b.shape[0]) for b in blocks]
    parts = [b[1:] for b in blocks]
    arrays = [b[0] for b in blocks]
    shape = (sum(stop - start for start, stop in parts), arrays[0].shape[1])
    loose = range(len(arrays), len(arrays) + len(needs))
    return call(functools.partial(pack_kernel, parts), single(*shape), [*arrays, *needs], loose=loose)


def unpack(whole, count):
    rows, cols = whole.shape
    return call(unpack_kernel, [single(rows // count, cols)] * count, [whole])


def on_device(reflect_fwd, transmit_fwd, reflect_bwd, transmit_bwd, material_ids, interface_gain):
    rows, cols = reflect_fwd.shape[1:]
    grid = Grid((rows, cols), *(lax.axis_size(a) for a in ("layer", "row", "col")))
    blocks, hops, cores, chips = grid.blocks, grid.hops, grid.cores, grid.chips
    order = rows * grid.row_count

    def plane(value, hop):
        route = []
        for layer in range(grid.layers):
            for row in range(grid.row_count):
                flip, on = hop[row % cores]
                target = (layer + grid.distance) % grid.layers if flip else layer
                route.append((layer * grid.row_count + row, target * grid.row_count + (row + on * cores) % grid.row_count))
        return lax.ppermute(value, ("layer", "row"), route)

    def both_cores(hop):
        return (hop, hop)

    def sibling(value):
        return lax.ppermute(value, "row", [(i, i ^ 1) for i in range(grid.row_count)])

    def ring(found, top=None):
        k = len(found)
        source = found[max(k - 2, 0)] if top is None else top
        shift = 1 if k % 2 else -1
        found.append(lax.ppermute(source, "col", [(i, (i + shift) % blocks) for i in range(blocks)]))

    def choose(first, second, *late):
        return call(
            functools.partial(choose_kernel, grid),
            single(rows, cols),
            [first, second, *late],
            far=(0, 1),
            loose=range(2, 2 + len(late)),
            scratch=[pltpu.SemaphoreType.DMA],
        )

    highs, lows, sums = [], [], []
    half = jax.ShapeDtypeStruct((2, order, cols), jnp.bfloat16)

    def absorb(pieces, new, height, weight, needs):
        nonlocal highs, lows, sums
        done = len(highs)
        operands = pieces + highs + lows + sums
        results = call(
            functools.partial(absorb_kernel, grid, done, new, height),
            [half] * (2 * new) + [single(order, cols)] * (done + new),
            operands + list(needs),
            loose=range(len(operands), len(operands) + len(needs)),
            aliases={len(operands) - done + n: 2 * new + n for n in range(done)},
            flops=int(weight * 6 * new * (2 * done + new) * order * cols * cols),
        )
        results = list(results)
        highs, lows, sums = highs + results[:new], lows + results[new : 2 * new], results[2 * new :]

    def along(value, shift):
        return lax.ppermute(value, "col", [(i, (i + shift) % blocks) for i in range(blocks)])

    def a_hop(value):
        return plane(value, hops[1])

    def b_hop(value):
        return plane(value, hops[2])

    upper_own = jnp.concatenate([reflect_bwd[0], transmit_bwd[0]], axis=0)
    lower_own = jnp.concatenate([reflect_fwd[0], transmit_fwd[0]], axis=0)
    values = {"q0": jnp.where(grid.upper(), upper_own, lower_own)}
    values["token"] = call(
        number_kernel,
        single(TILE, cols),
        [material_ids],
        far=(0,),
        scratch=[pltpu.SMEM(material_ids.shape, jnp.int32), pltpu.SemaphoreType.DMA],
    )
    end = 2 * rows + TILE
    up, down = functools.partial(along, shift=1), functools.partial(along, shift=-1)
    moves = {
        "p1": (up, "p0"),
        "q2": (down, "q0"),
        "q3": (up, "r1"),
        "l3": (up, "l1"),
        **{f"a{i}": (a_hop, "e1" if i == 1 else f"p{i}") for i in range(4)},
        **{f"b{i}": (b_hop, "e1" if i == 1 else f"p{i}") for i in range(4)},
        **{f"d{i}": (b_hop, f"a{i}") for i in range(4)},
        **{f"t{m}": (sibling, f"m{m}") for m in ("01", "2", "3", "x")},
    }

    def head(name):
        return (values[name], 0, rows)

    def tail(name, stop):
        return (values[name], rows, stop)

    def packed(*names):
        return names, lambda: pack([head(n) for n in names])

    made = {
        "e1": (("p1",), lambda: call(extend_kernel, single(end, cols), [values["p1"], transmit_fwd, values["token"]])),
        "r1": (("p1",), lambda: pack([values["p1"], tail("q0", 2 * rows)])),
        "l1": (("q3",), lambda: pack([tail("q3", 2 * rows)])),
        "p0": packed("q0"),
        "p2": packed("q2"),
        "p3": packed("q3"),
        "m01": packed("q0", "p1", "a0", "a1", "b0", "b1", "d0", "d1"),
        "m2": packed("q2", "a2", "b2", "d2"),
        "m3": packed("q3", "a3", "b3", "d3"),
        "mx": (("a1", "b1", "d1"), lambda: pack([tail(n, end) for n in ("e1", "a1", "b1", "d1")])),
    }
    kernels = {"01": (2, 2 * rows), "2": (1, rows)}

    def absorb_named(name):
        new, height = kernels[name]
        absorb([values[f"m{name}"], values[f"t{name}"]], new, height, 1, [])

    def pass_gate(gate_number, *needs):
        starting = [t for t in SLOTS if t in moves and SLOTS[t][0] == gate_number]
        ending = [t for t in SLOTS if t in moves and SLOTS[t][1] == gate_number]
        needs = list(needs)
        for name, number in KERNELS.items():
            if number == gate_number:
                absorb_named(name)
                needs.append(highs[-1])
        passed = ["token"]
        for t in starting:
            source = moves[t][1]
            if source not in values:
                sources = made[source][0]
                source = max(sources, key=lambda n: SLOTS[n][1] if n in SLOTS else -1) if sources else "token"
            if source not in passed:
                passed.append(source)
        needs += [values[t] for t in ending if t not in passed]
        for name, value in zip(passed, gate([values[n] for n in passed], *needs)):
            values[name] = value
        for t in starting:
            function, source = moves[t]
            if source not in values:
                values[source] = made[source][1]()
            with jax.named_scope(t):
                values[t] = function(values[source])

    for gate_number in range(ANCHOR + 1):
        pass_gate(gate_number)
    for name in ("01", "2"):
        if name not in KERNELS:
            absorb_named(name)
    panel, weight = call(
        functools.partial(panel_kernel, grid, 0),
        [single(order, cols), single(-(-order // cols // TILE) * TILE, cols)],
        [interface_gain, values["mx"], values["tx"]],
    )
    width = cols // cores
    operands = [values["m3"], values["t3"], *highs, *lows, *sums, panel]
    part, high, low = call(
        functools.partial(horner_kernel, grid),
        [single(order, width), half, half],
        [*operands, values["token"]],
        loose=(len(operands),),
        scratch=[pltpu.VMEM((order, order), jnp.bfloat16)] * 2 + [pltpu.VMEM((order, 2 * width), jnp.bfloat16)],
        flops=10 * 6 * NTERMS * order * order * width,
        limit=10 * MIB,
    )
    highs, lows = highs + [high], lows + [low]
    parts = [part] + ([sibling(part)] if cores == 2 else [])
    for gate_number in range(ANCHOR + 1, 1 + max(t[1] for t in SLOTS.values())):
        pass_gate(gate_number, part)
    left = [values[n] for n in ("q0", "q3", "q2", "l3")]
    operands = highs + lows + left + [weight]
    left = call(
        functools.partial(left_kernel, grid),
        [jax.ShapeDtypeStruct((rows, order), jnp.bfloat16)] * 2,
        [*operands, values["token"]],
        loose=(len(operands),),
        flops=6 * rows * order * order,
    )
    result = call(
        functools.partial(last_kernel, grid),
        single(rows, cols),
        [*left, reflect_fwd, *parts],
        scratch=[pltpu.VMEM((order, cols), jnp.bfloat16)] * 2,
        flops=6 * rows * order * cols,
    )
    across = plane(result, both_cores((1, 0)))
    outs = [single(1, rows, cols)] * 2
    return tuple(call(functools.partial(finish_kernel, grid), outs, [result, across]))


def solution(mesh):
    block = P("layer", "row", "col")
    return jax.shard_map(
        on_device,
        mesh=mesh,
        in_specs=(block, block, block, block, P("layer"), P()),
        out_specs=(block, block),
        check_vma=False,
    )
```

```python
import functools

import jax
import jax.numpy as jnp
from jax import lax
from jax.experimental import pallas as pl
from jax.experimental.pallas import tpu as pltpu
from jax.sharding import PartitionSpec as P

NTERMS = 6
MIB = 2**20
TILE = 8
GATE = 2 * 10**10

SLOTS = {
    "p1": (1, 3),
    "a0": (0, 2),
    "b0": (1, 3),
    "xx": (1, 3),
    "p2": (2, 4),
    "d0": (2, 4),
    "a1": (3, 5),
    "b1": (4, 7),
    "p3": (3, 5),
    "a2": (4, 6),
    "xy": (3, 5),
    "d1": (5, 7),
    "a3": (5, 7),
    "d2": (6, 8),
    "b2": (6, 8),
    "b3": (7, 9),
    "d3": (7, 10),
    "t01": (7, 9),
    "tx": (8, 10),
    "t2": (8, 10),
    "td": (10, 11),
    "l1": (9, 11),
    "t3": (9, 11),
    "l2": (10, 12),
    "l3": (11, 12),
}
KERNELS = {'01': 9, '2': 10}
DIAGONAL = {'d1': 'p', 'd2': 'z', 'd3': 'p'}
ANCHOR = 11


class Grid:
    def __init__(self, shape, layers, row_count, blocks):
        self.shape = shape
        self.layers, self.row_count, self.blocks = layers, row_count, blocks
        self.distance = layers // 2
        self.cores = 2 if row_count % 2 == 0 else 1
        self.chips = row_count // self.cores
        self.hops = [((0, 0), (0, 0))]
        if self.chips == 2:
            self.hops += [((1, 0), (0, 1)), ((0, 1), (1, 0)), ((1, 1), (1, 1))]
        else:
            self.hops += [((1, 0), (1, 0))]
            self.hops += [((f, h), (f, h)) for f in (0, 1) for h in range(1, self.chips)]

    def upper(self):
        return lax.axis_index("layer") < self.distance

    def row(self):
        return lax.axis_index("row")

    def place(self, k):
        hop = k // 2 if k % 2 == 0 else self.blocks - k // 2 - 1
        return lax.rem(lax.axis_index("col") + hop, self.blocks)

    def row_of(self, hop, other):
        row = self.row()
        core = lax.rem(row, self.cores)
        chip = lax.rem(lax.div(row, self.cores) + self.chips - hop, self.chips)
        return chip * self.cores + (self.cores - 1 - core if other else core)

    def origins(self):
        side = jnp.where(self.upper(), 0, 1)
        odd = lax.rem(self.row(), self.cores)
        found = []
        for other in range(self.cores):
            for even_hop, odd_hop in self.hops:
                on_odd = (1 - odd if other else odd) == 1
                flip = jnp.where(on_odd, odd_hop[0], even_hop[0])
                hop = jnp.where(on_odd, odd_hop[1], even_hop[1])
                found.append((jnp.where(flip == 1, 1 - side, side), self.row_of(hop, other)))
        return found


def split(value):
    high = value.astype(jnp.bfloat16)
    return high, (value - high.astype(jnp.float32)).astype(jnp.bfloat16)


def dot(left, right):
    return jnp.dot(left, right, preferred_element_type=jnp.float32)


def dot3(left_high, left_low, right_high, right_low):
    return dot(left_high, right_high) + (dot(left_high, right_low) + dot(left_low, right_high))


def span(index, size):
    return pl.ds(pl.multiple_of(index * size, size), size)


def extend_kernel(ids, block, late, out, number, sem):
    del late
    rows = block.shape[1]
    copy = pltpu.make_async_copy(ids, number, sem)
    copy.start()
    out[:rows, :] = block[0]
    copy.wait()
    out[rows:, :] = jnp.full((TILE, out.shape[1]), number[0].astype(jnp.float32))


def scale_kernel(grid, own, across, gains, panel, weight):
    rows, cols = grid.shape

    def gain(block, i):
        number = block[rows : rows + 1, :]
        here = pl.ds(i * cols, cols)
        return sum(jnp.where(number == m, gains[m : m + 1, here], 0.0) for m in range(gains.shape[0]))

    for i in range(gains.shape[1] // cols):
        weight[i : i + 1, :] = gain(own, i) * gain(across, i)
    here = weight[pl.ds(lax.div(grid.row() * rows, cols), 1), :]
    column = jnp.concatenate([here] * 8, axis=0).T[:, :1]
    panel[...] = jnp.where(grid.upper(), own[:rows, :], across[:rows, :]) * column


def gate_kernel(count, *refs):
    for value, out in zip(refs[:count], refs[-count:]):
        out[...] = value[...]


def pack_kernel(parts, *refs):
    here = 0
    for ref, (start, stop) in zip(refs, parts):
        refs[-1][here : here + stop - start, :] = ref[start:stop, :]
        here += stop - start


def ingest(grid, refs, new, height, highs, lows):
    rows = grid.shape[0]
    pieces = [ref.at[pl.ds(i, height), :] for ref in refs for i in range(0, ref.shape[0], height)]
    for piece, (side, row) in zip(pieces, grid.origins()):
        for j in range(new):
            high, low = split(piece[j * rows : (j + 1) * rows, :])
            highs[j][side, span(row, rows), :] = high
            lows[j][side, span(row, rows), :] = low


def absorb_kernel(grid, done, new, height, mine, theirs, *refs):
    cols = grid.shape[1]
    old, sums = refs[: 2 * done], refs[2 * done : 3 * done]
    refs = refs[-(3 * new + done) :]
    fresh, out_sums = refs[: 2 * new], refs[2 * new :]
    highs, lows = old[:done] + fresh[:new], old[done:] + fresh[new:]
    ingest(grid, [mine, theirs], new, height, fresh[:new], fresh[new:])
    for n in range(done + new):
        total = sums[n][...] if n < done else None
        for k in range(done if n < done else 0, done + new):
            here = span(grid.place(k), cols)
            term = dot3(highs[k][0], lows[k][0], highs[n][1, here, :], lows[n][1, here, :])
            total = term if total is None else total + term
        out_sums[n][...] = total


def horner_kernel(grid, *refs):
    rows, cols = grid.shape
    blocks = grid.blocks
    old = blocks - 1
    last, refs = refs[:4], refs[4:]
    highs, lows, sums, refs = refs[:old], refs[old : 2 * old], refs[2 * old : 3 * old], refs[3 * old :]
    mine_x, theirs_x, _, out, high, low, power_high, power_low, pair, base = refs
    width = out.shape[1]
    ingest(grid, last, 1, rows, [high], [low])
    highs, lows = (*highs, high), (*lows, low)
    places = [grid.place(j) for j in range(blocks)]
    for n in range(blocks):
        total = sums[n][...] if n < old else None
        for k in range(old if n < old else 0, blocks):
            here = span(places[k], cols)
            term = dot3(highs[k][0], lows[k][0], highs[n][1, here, :], lows[n][1, here, :])
            total = term if total is None else total + term
        here = pl.ds(n * cols, cols)
        power_high[:, here], power_low[:, here] = split(total)

    ours = span(lax.rem(grid.row(), grid.cores), width)

    def take(read):
        for j in range(blocks):
            z_high, z_low = split(read(span(places[j], cols)))
            here = pl.ds(j * cols, cols)
            pair[here, :width], pair[here, width:] = z_high, z_low

    pieces = [ref.at[pl.ds(i, rows), :] for ref in (mine_x, theirs_x) for i in range(0, ref.shape[0], rows)]
    starts = [grid.row_of(hop, other) for other in range(grid.cores) for hop in range(grid.chips)]
    for piece, start in zip(pieces, starts):
        base[span(start, rows), :] = piece[:, ours]
    take(lambda here: base[here, :])

    @pl.loop(0, NTERMS - 1)
    def _(_):
        both = dot(power_high[...], pair[...])
        rest = dot(power_low[...], pair[:, :width])
        out[...] = base[...] + (both[:, :width] + (both[:, width:] + rest))
        take(lambda here: out[here, :])


def left_kernel(grid, *refs):
    blocks = grid.blocks
    highs, lows, left, (weight, _, left_high, left_low) = refs[:blocks], refs[blocks : 2 * blocks], refs[2 * blocks : 3 * blocks], refs[3 * blocks :]
    rows, cols = grid.shape
    places = [grid.place(j) for j in range(blocks)]
    left = [ref.at[pl.ds(ref.shape[0] - rows, rows), :] for ref in left]

    @pl.when(grid.upper())
    def _():
        scaled = [split(left[j][...] * weight[pl.ds(places[j], 1), :]) for j in range(blocks)]
        for n in range(blocks):
            total = None
            for j in range(blocks):
                term = dot3(*scaled[j], highs[n][1, span(places[j], cols), :], lows[n][1, span(places[j], cols), :])
                total = term if total is None else total + term
            here = pl.ds(n * cols, cols)
            left_high[:, here], left_low[:, here] = split(total)

    @pl.when(jnp.logical_not(grid.upper()))
    def _():
        for n in range(blocks):
            here = pl.ds(n * cols, cols)
            left_high[:, here], left_low[:, here] = split(left[n][...])


def last_kernel(grid, left_high, left_low, reflect, *refs):
    parts, (out, z_high, z_low) = refs[:-3], refs[-3:]
    cols = grid.shape[1]
    width = parts[0].shape[1]
    core = lax.rem(grid.row(), grid.cores)
    for i, part in enumerate(parts):
        ours = span(core if i == 0 else 1 - core, width)
        for j in range(grid.blocks):
            here = pl.ds(j * cols, cols)
            z_high[here, ours], z_low[here, ours] = split(part[span(grid.place(j), cols), :])
    result = dot3(left_high[...], left_low[...], z_high[...], z_low[...])
    out[...] = jnp.where(grid.upper(), reflect[0] + result, result)


def finish_kernel(grid, own, across, reflect, transmit):
    upper = grid.upper()
    reflect[0] = jnp.where(upper, own[...], across[...])
    transmit[0] = jnp.where(upper, across[...], own[...])


def call(kernel, outs, operands, scalars=(), loose=(), far=(), scratch=(), aliases=None, flops=0, moved=0, limit=4 * MIB):
    spaces = [pltpu.VMEM] * len(operands)
    for numbers, space in ((scalars, pltpu.SMEM), (far, pltpu.HBM), (loose, pl.ANY)):
        for i in numbers:
            spaces[i] = space
    specs = [pl.BlockSpec(memory_space=space) for space in spaces]
    return pl.pallas_call(
        kernel,
        out_shape=outs,
        in_specs=specs,
        out_specs=jax.tree.map(lambda _: pl.BlockSpec(memory_space=pltpu.VMEM), outs),
        scratch_shapes=list(scratch),
        input_output_aliases=aliases or {},
        compiler_params=pltpu.CompilerParams(vmem_limit_bytes=limit),
        cost_estimate=pl.CostEstimate(flops=flops, bytes_accessed=moved, transcendentals=0),
    )(*operands)


def single(*shape):
    return jax.ShapeDtypeStruct(shape, jnp.float32)


def gate(values, *needs):
    count = len(values)
    kernel = functools.partial(gate_kernel, count)
    return call(kernel, [single(*v.shape) for v in values], [*values, *needs], loose=range(count, count + len(needs)), flops=GATE, moved=10 * GATE)


def pack(blocks, *needs):
    blocks = [b if isinstance(b, tuple) else (b, 0, b.shape[0]) for b in blocks]
    parts = [b[1:] for b in blocks]
    arrays = [b[0] for b in blocks]
    shape = (sum(stop - start for start, stop in parts), arrays[0].shape[1])
    loose = range(len(arrays), len(arrays) + len(needs))
    return call(functools.partial(pack_kernel, parts), single(*shape), [*arrays, *needs], loose=loose)


def on_device(reflect_fwd, transmit_fwd, reflect_bwd, transmit_bwd, material_ids, interface_gain):
    rows, cols = reflect_fwd.shape[1:]
    grid = Grid((rows, cols), *(lax.axis_size(a) for a in ("layer", "row", "col")))
    blocks, hops, cores, chips = grid.blocks, grid.hops, grid.cores, grid.chips
    order = rows * grid.row_count

    def plane(value, hop):
        route = []
        for layer in range(grid.layers):
            for row in range(grid.row_count):
                flip, on = hop[row % cores]
                target = (layer + grid.distance) % grid.layers if flip else layer
                route.append((layer * grid.row_count + row, target * grid.row_count + (row + on * cores) % grid.row_count))
        return lax.ppermute(value, ("layer", "row"), route)

    def both_cores(hop):
        return (hop, hop)

    def sibling(value):
        return lax.ppermute(value, "row", [(i, i ^ 1) for i in range(grid.row_count)])

    def ring(found, top=None):
        k = len(found)
        source = found[max(k - 2, 0)] if top is None else top
        shift = 1 if k % 2 else -1
        found.append(lax.ppermute(source, "col", [(i, (i + shift) % blocks) for i in range(blocks)]))

    highs, lows, sums = [], [], []
    half = jax.ShapeDtypeStruct((2, order, cols), jnp.bfloat16)

    def absorb(pieces, new, height, weight, needs):
        nonlocal highs, lows, sums
        done = len(highs)
        operands = pieces + highs + lows + sums
        results = call(
            functools.partial(absorb_kernel, grid, done, new, height),
            [half] * (2 * new) + [single(order, cols)] * (done + new),
            operands + list(needs),
            loose=range(len(operands), len(operands) + len(needs)),
            aliases={len(operands) - done + n: 2 * new + n for n in range(done)},
            flops=int(weight * 6 * new * (2 * done + new) * order * cols * cols),
        )
        results = list(results)
        highs, lows, sums = highs + results[:new], lows + results[new : 2 * new], results[2 * new :]

    def along(value, shift):
        return lax.ppermute(value, "col", [(i, (i + shift) % blocks) for i in range(blocks)])

    def a_hop(value):
        return plane(value, hops[1])

    def b_hop(value):
        return plane(value, hops[2])

    upper_own = jnp.concatenate([reflect_bwd[0], transmit_bwd[0]], axis=0)
    lower_own = jnp.concatenate([reflect_fwd[0], transmit_fwd[0]], axis=0)
    values = {"q0": jnp.where(grid.upper(), upper_own, lower_own)}
    values["token"] = pack([(values["q0"], 0, TILE)])
    up, down = functools.partial(along, shift=1), functools.partial(along, shift=-1)
    flip, over = (functools.partial(plane, hop=both_cores(hop)) for hop in ((1, 0), (0, 1)))
    moves = {
        "p1": (up, "p0"),
        "p2": (down, "p0"),
        "p3": (up, "p1"),
        "l1": (up, "l0"),
        "l2": (down, "l0"),
        "l3": (up, "l1"),
        **{f"a{i}": (a_hop, f"p{i}") for i in range(4)},
        **{f"b{i}": (b_hop, f"p{i}") for i in range(4)},
        "d0": (b_hop, "a0"),
        "d1": (up, "d0") if DIAGONAL["d1"] == "z" else (b_hop, "a1"),
        "d2": (down, "d0") if DIAGONAL["d2"] == "z" else (b_hop, "a2"),
        "d3": (up, "d1") if DIAGONAL["d3"] == "z" else (b_hop, "a3"),
        **{f"t{m}": (sibling, f"m{m}") for m in ("01", "2", "3", "x")},
        "td": (sibling, "d3"),
        "xx": (flip, "x0"),
        "xy": (over, "x1"),
    }

    def packed(*names):
        return names, lambda: pack([values[n] for n in names])

    def extend():
        return call(
            extend_kernel,
            single(rows + TILE, cols),
            [material_ids, transmit_fwd, values["token"]],
            far=(0,),
            loose=(2,),
            scratch=[pltpu.SMEM(material_ids.shape, jnp.int32), pltpu.SemaphoreType.DMA],
        )

    def scale():
        outs = [single(rows, cols), single(-(-order // cols // TILE) * TILE, cols)]
        operands = [values["x0"], values["xx"], interface_gain]
        panel, values["weight"] = call(functools.partial(scale_kernel, grid), outs, operands)
        return panel

    made = {
        "p0": ((), lambda: pack([(values["q0"], 0, rows)])),
        "l0": ((), lambda: pack([(values["q0"], rows, 2 * rows)])),
        "x0": ((), extend),
        "x1": (("xx",), scale),
        "m01": packed("p0", "p1", "a0", "a1", "b0", "b1", "d0", "d1"),
        "m2": packed("p2", "a2", "b2", "d2"),
        "m3": packed("p3", "a3", "b3"),
        "mx": packed("x1", "xy"),
    }
    kernels = {"01": (2, 2 * rows), "2": (1, rows)}

    def absorb_named(name):
        new, height = kernels[name]
        absorb([values[f"m{name}"], values[f"t{name}"]], new, height, 1, [])

    def pass_gate(gate_number, *needs):
        starting = [t for t in SLOTS if t in moves and SLOTS[t][0] == gate_number]
        ending = [t for t in SLOTS if t in moves and SLOTS[t][1] == gate_number]
        needs = list(needs)
        for name, number in KERNELS.items():
            if number == gate_number:
                absorb_named(name)
                needs.append(highs[-1])
        passed = ["token"]
        for t in starting:
            source = moves[t][1]
            if source not in values:
                sources = made[source][0]
                source = max(sources, key=lambda n: SLOTS[n][1] if n in SLOTS else -1) if sources else "token"
            if source not in passed:
                passed.append(source)
        needs += [values[t] for t in ending if t not in passed]
        for name, value in zip(passed, gate([values[n] for n in passed], *needs)):
            values[name] = value
        for t in starting:
            function, source = moves[t]
            if source not in values:
                values[source] = made[source][1]()
            with jax.named_scope(t):
                values[t] = function(values[source])

    for gate_number in range(ANCHOR + 1):
        pass_gate(gate_number)
    for name in ("01", "2"):
        if name not in KERNELS:
            absorb_named(name)
    width = cols // cores
    operands = [values[n] for n in ("m3", "d3", "t3", "td")] + [*highs, *lows, *sums, values["mx"], values["tx"]]
    part, high, low = call(
        functools.partial(horner_kernel, grid),
        [single(order, width), half, half],
        [*operands, values["token"]],
        loose=(len(operands),),
        scratch=[pltpu.VMEM((order, order), jnp.bfloat16)] * 2 + [pltpu.VMEM((order, 2 * width), jnp.bfloat16), pltpu.VMEM((order, width), jnp.float32)],
        flops=10 * 6 * NTERMS * order * order * width,
        limit=10 * MIB,
    )
    highs, lows = highs + [high], lows + [low]
    parts = [part] + ([sibling(part)] if cores == 2 else [])
    for gate_number in range(ANCHOR + 1, 1 + max(t[1] for t in SLOTS.values())):
        pass_gate(gate_number, part)
    left = [values[n] for n in ("l0", "l1", "l2", "l3")]
    operands = highs + lows + left + [values["weight"]]
    left = call(
        functools.partial(left_kernel, grid),
        [jax.ShapeDtypeStruct((rows, order), jnp.bfloat16)] * 2,
        [*operands, values["token"]],
        loose=(len(operands),),
        flops=6 * rows * order * order,
    )
    result = call(
        functools.partial(last_kernel, grid),
        single(rows, cols),
        [*left, reflect_fwd, *parts],
        scratch=[pltpu.VMEM((order, cols), jnp.bfloat16)] * 2,
        flops=6 * rows * order * cols,
    )
    across = plane(result, both_cores((1, 0)))
    outs = [single(1, rows, cols)] * 2
    return tuple(call(functools.partial(finish_kernel, grid), outs, [result, across]))


def solution(mesh):
    block = P("layer", "row", "col")
    return jax.shard_map(
        on_device,
        mesh=mesh,
        in_specs=(block, block, block, block, P("layer"), P()),
        out_specs=(block, block),
        check_vma=False,
    )
```

```python
import functools

import jax
import jax.numpy as jnp
from jax import lax
from jax.experimental import pallas as pl
from jax.experimental.pallas import tpu as pltpu
from jax.sharding import PartitionSpec as P

NTERMS = 6
MIB = 2**20
TILE = 8
GATE = 2 * 10**10

SLOTS = {
    "p1": (1, 3),
    "a0": (0, 2),
    "b0": (0, 2),
    "t01": (7, 9),
    "xx": (1, 3),
    "p2": (2, 4),
    "d0": (2, 4),
    "a1": (3, 5),
    "b1": (4, 7),
    "p3": (3, 5),
    "xy": (3, 5),
    "d1": (5, 7),
    "a3": (5, 7),
    "d2": (6, 8),
    "b2": (6, 8),
    "b3": (7, 9),
    "d3": (7, 10),
    "t2": (8, 10),
    "td": (10, 11),
    "l1": (9, 11),
    "t3": (9, 11),
    "tx": (8, 10),
    "a2": (4, 6),
    "l2": (10, 12),
    "l3": (11, 12),
}
KERNELS = {'01': 9, '2': 10}
DIAGONAL = {'d1': 'p', 'd2': 'z', 'd3': 'p'}
ANCHOR = 11


class Grid:
    def __init__(self, shape, layers, row_count, blocks):
        self.shape = shape
        self.layers, self.row_count, self.blocks = layers, row_count, blocks
        self.distance = layers // 2
        self.cores = 2 if row_count % 2 == 0 else 1
        self.chips = row_count // self.cores
        self.hops = [((0, 0), (0, 0))]
        if self.chips == 2:
            self.hops += [((1, 0), (0, 1)), ((0, 1), (1, 0)), ((1, 1), (1, 1))]
        else:
            self.hops += [((1, 0), (1, 0))]
            self.hops += [((f, h), (f, h)) for f in (0, 1) for h in range(1, self.chips)]

    def upper(self):
        return lax.axis_index("layer") < self.distance

    def row(self):
        return lax.axis_index("row")

    def place(self, k):
        hop = k // 2 if k % 2 == 0 else self.blocks - k // 2 - 1
        return lax.rem(lax.axis_index("col") + hop, self.blocks)

    def row_of(self, hop, other):
        row = self.row()
        core = lax.rem(row, self.cores)
        chip = lax.rem(lax.div(row, self.cores) + self.chips - hop, self.chips)
        return chip * self.cores + (self.cores - 1 - core if other else core)

    def origins(self):
        side = jnp.where(self.upper(), 0, 1)
        odd = lax.rem(self.row(), self.cores)
        found = []
        for other in range(self.cores):
            for even_hop, odd_hop in self.hops:
                on_odd = (1 - odd if other else odd) == 1
                flip = jnp.where(on_odd, odd_hop[0], even_hop[0])
                hop = jnp.where(on_odd, odd_hop[1], even_hop[1])
                found.append((jnp.where(flip == 1, 1 - side, side), self.row_of(hop, other)))
        return found


def split(value):
    high = value.astype(jnp.bfloat16)
    return high, (value - high.astype(jnp.float32)).astype(jnp.bfloat16)


def dot(left, right):
    return jnp.dot(left, right, preferred_element_type=jnp.float32)


def dot3(left_high, left_low, right_high, right_low):
    return dot(left_high, right_high) + (dot(left_high, right_low) + dot(left_low, right_high))


def span(index, size):
    return pl.ds(pl.multiple_of(index * size, size), size)


def extend_kernel(ids, block, late, out, number, sem):
    del late
    rows = block.shape[1]
    copy = pltpu.make_async_copy(ids, number, sem)
    copy.start()
    out[:rows, :] = block[0]
    copy.wait()
    out[rows:, :] = jnp.full((TILE, out.shape[1]), number[0].astype(jnp.float32))


def scale_kernel(grid, own, across, gains, panel, weight):
    rows, cols = grid.shape

    def gain(block, i):
        number = block[rows : rows + 1, :]
        here = pl.ds(i * cols, cols)
        return sum(jnp.where(number == m, gains[m : m + 1, here], 0.0) for m in range(gains.shape[0]))

    for i in range(gains.shape[1] // cols):
        weight[i : i + 1, :] = gain(own, i) * gain(across, i)
    here = weight[pl.ds(lax.div(grid.row() * rows, cols), 1), :]
    column = jnp.concatenate([here] * 8, axis=0).T[:, :1]
    panel[...] = jnp.where(grid.upper(), own[:rows, :], across[:rows, :]) * column


def gate_kernel(count, *refs):
    for value, out in zip(refs[:count], refs[-count:]):
        out[...] = value[...]


def pack_kernel(parts, *refs):
    here = 0
    for ref, (start, stop) in zip(refs, parts):
        refs[-1][here : here + stop - start, :] = ref[start:stop, :]
        here += stop - start


def ingest(grid, refs, new, height, highs, lows):
    rows = grid.shape[0]
    pieces = [ref.at[pl.ds(i, height), :] for ref in refs for i in range(0, ref.shape[0], height)]
    for piece, (side, row) in zip(pieces, grid.origins()):
        for j in range(new):
            high, low = split(piece[j * rows : (j + 1) * rows, :])
            highs[j][side, span(row, rows), :] = high
            lows[j][side, span(row, rows), :] = low


def absorb_kernel(grid, done, new, height, mine, theirs, *refs):
    cols = grid.shape[1]
    old, sums = refs[: 2 * done], refs[2 * done : 3 * done]
    refs = refs[-(3 * new + done) :]
    fresh, out_sums = refs[: 2 * new], refs[2 * new :]
    highs, lows = old[:done] + fresh[:new], old[done:] + fresh[new:]
    ingest(grid, [mine, theirs], new, height, fresh[:new], fresh[new:])
    for n in range(done + new):
        total = sums[n][...] if n < done else None
        for k in range(done if n < done else 0, done + new):
            here = span(grid.place(k), cols)
            term = dot3(highs[k][0], lows[k][0], highs[n][1, here, :], lows[n][1, here, :])
            total = term if total is None else total + term
        out_sums[n][...] = total


def horner_kernel(grid, *refs):
    rows, cols = grid.shape
    blocks = grid.blocks
    old = blocks - 1
    last, refs = refs[:4], refs[4:]
    highs, lows, sums, refs = refs[:old], refs[old : 2 * old], refs[2 * old : 3 * old], refs[3 * old :]
    mine_x, theirs_x, _, out, high, low, power_high, power_low, pair, base = refs
    width = out.shape[1]
    ingest(grid, last, 1, rows, [high], [low])
    highs, lows = (*highs, high), (*lows, low)
    places = [grid.place(j) for j in range(blocks)]
    for n in range(blocks):
        total = sums[n][...] if n < old else None
        for k in range(old if n < old else 0, blocks):
            here = span(places[k], cols)
            term = dot3(highs[k][0], lows[k][0], highs[n][1, here, :], lows[n][1, here, :])
            total = term if total is None else total + term
        here = pl.ds(n * cols, cols)
        power_high[:, here], power_low[:, here] = split(total)

    ours = span(lax.rem(grid.row(), grid.cores), width)

    def take(read):
        for j in range(blocks):
            z_high, z_low = split(read(span(places[j], cols)))
            here = pl.ds(j * cols, cols)
            pair[here, :width], pair[here, width:] = z_high, z_low

    pieces = [ref.at[pl.ds(i, rows), :] for ref in (mine_x, theirs_x) for i in range(0, ref.shape[0], rows)]
    starts = [grid.row_of(hop, other) for other in range(grid.cores) for hop in range(grid.chips)]
    for piece, start in zip(pieces, starts):
        base[span(start, rows), :] = piece[:, ours]
    take(lambda here: base[here, :])

    @pl.loop(0, NTERMS - 1)
    def _(_):
        both = dot(power_high[...], pair[...])
        rest = dot(power_low[...], pair[:, :width])
        out[...] = base[...] + (both[:, :width] + (both[:, width:] + rest))
        take(lambda here: out[here, :])


def left_kernel(grid, *refs):
    blocks = grid.blocks
    highs, lows, left, (weight, _, left_high, left_low) = refs[:blocks], refs[blocks : 2 * blocks], refs[2 * blocks : 3 * blocks], refs[3 * blocks :]
    rows, cols = grid.shape
    places = [grid.place(j) for j in range(blocks)]
    left = [ref.at[pl.ds(ref.shape[0] - rows, rows), :] for ref in left]

    @pl.when(grid.upper())
    def _():
        scaled = [split(left[j][...] * weight[pl.ds(places[j], 1), :]) for j in range(blocks)]
        for n in range(blocks):
            total = None
            for j in range(blocks):
                term = dot3(*scaled[j], highs[n][1, span(places[j], cols), :], lows[n][1, span(places[j], cols), :])
                total = term if total is None else total + term
            here = pl.ds(n * cols, cols)
            left_high[:, here], left_low[:, here] = split(total)

    @pl.when(jnp.logical_not(grid.upper()))
    def _():
        for n in range(blocks):
            here = pl.ds(n * cols, cols)
            left_high[:, here], left_low[:, here] = split(left[n][...])


def last_kernel(grid, left_high, left_low, reflect, *refs):
    parts, (out, z_high, z_low) = refs[:-3], refs[-3:]
    cols = grid.shape[1]
    width = parts[0].shape[1]
    core = lax.rem(grid.row(), grid.cores)
    for i, part in enumerate(parts):
        ours = span(core if i == 0 else 1 - core, width)
        for j in range(grid.blocks):
            here = pl.ds(j * cols, cols)
            z_high[here, ours], z_low[here, ours] = split(part[span(grid.place(j), cols), :])
    result = dot3(left_high[...], left_low[...], z_high[...], z_low[...])
    out[...] = jnp.where(grid.upper(), reflect[0] + result, result)


def finish_kernel(grid, own, across, reflect, transmit):
    upper = grid.upper()
    reflect[0] = jnp.where(upper, own[...], across[...])
    transmit[0] = jnp.where(upper, across[...], own[...])


def call(kernel, outs, operands, scalars=(), loose=(), far=(), scratch=(), aliases=None, flops=0, moved=0, limit=4 * MIB):
    spaces = [pltpu.VMEM] * len(operands)
    for numbers, space in ((scalars, pltpu.SMEM), (far, pltpu.HBM), (loose, pl.ANY)):
        for i in numbers:
            spaces[i] = space
    specs = [pl.BlockSpec(memory_space=space) for space in spaces]
    return pl.pallas_call(
        kernel,
        out_shape=outs,
        in_specs=specs,
        out_specs=jax.tree.map(lambda _: pl.BlockSpec(memory_space=pltpu.VMEM), outs),
        scratch_shapes=list(scratch),
        input_output_aliases=aliases or {},
        compiler_params=pltpu.CompilerParams(vmem_limit_bytes=limit),
        cost_estimate=pl.CostEstimate(flops=flops, bytes_accessed=moved, transcendentals=0),
    )(*operands)


def single(*shape):
    return jax.ShapeDtypeStruct(shape, jnp.float32)


def gate(values, *needs):
    count = len(values)
    kernel = functools.partial(gate_kernel, count)
    return call(kernel, [single(*v.shape) for v in values], [*values, *needs], loose=range(count, count + len(needs)), flops=GATE, moved=10 * GATE)


def pack(blocks, *needs):
    blocks = [b if isinstance(b, tuple) else (b, 0, b.shape[0]) for b in blocks]
    parts = [b[1:] for b in blocks]
    arrays = [b[0] for b in blocks]
    shape = (sum(stop - start for start, stop in parts), arrays[0].shape[1])
    loose = range(len(arrays), len(arrays) + len(needs))
    return call(functools.partial(pack_kernel, parts), single(*shape), [*arrays, *needs], loose=loose)


def on_device(reflect_fwd, transmit_fwd, reflect_bwd, transmit_bwd, material_ids, interface_gain):
    rows, cols = reflect_fwd.shape[1:]
    grid = Grid((rows, cols), *(lax.axis_size(a) for a in ("layer", "row", "col")))
    blocks, hops, cores, chips = grid.blocks, grid.hops, grid.cores, grid.chips
    order = rows * grid.row_count

    def plane(value, hop):
        route = []
        for layer in range(grid.layers):
            for row in range(grid.row_count):
                flip, on = hop[row % cores]
                target = (layer + grid.distance) % grid.layers if flip else layer
                route.append((layer * grid.row_count + row, target * grid.row_count + (row + on * cores) % grid.row_count))
        return lax.ppermute(value, ("layer", "row"), route)

    def both_cores(hop):
        return (hop, hop)

    def sibling(value):
        return lax.ppermute(value, "row", [(i, i ^ 1) for i in range(grid.row_count)])

    def ring(found, top=None):
        k = len(found)
        source = found[max(k - 2, 0)] if top is None else top
        shift = 1 if k % 2 else -1
        found.append(lax.ppermute(source, "col", [(i, (i + shift) % blocks) for i in range(blocks)]))

    highs, lows, sums = [], [], []
    half = jax.ShapeDtypeStruct((2, order, cols), jnp.bfloat16)

    def absorb(pieces, new, height, weight, needs):
        nonlocal highs, lows, sums
        done = len(highs)
        operands = pieces + highs + lows + sums
        results = call(
            functools.partial(absorb_kernel, grid, done, new, height),
            [half] * (2 * new) + [single(order, cols)] * (done + new),
            operands + list(needs),
            loose=range(len(operands), len(operands) + len(needs)),
            aliases={len(operands) - done + n: 2 * new + n for n in range(done)},
            flops=int(weight * 6 * new * (2 * done + new) * order * cols * cols),
        )
        results = list(results)
        highs, lows, sums = highs + results[:new], lows + results[new : 2 * new], results[2 * new :]

    def along(value, shift):
        return lax.ppermute(value, "col", [(i, (i + shift) % blocks) for i in range(blocks)])

    def a_hop(value):
        return plane(value, hops[1])

    def b_hop(value):
        return plane(value, hops[2])

    upper_own = jnp.concatenate([reflect_bwd[0], transmit_bwd[0]], axis=0)
    lower_own = jnp.concatenate([reflect_fwd[0], transmit_fwd[0]], axis=0)
    values = {"q0": jnp.where(grid.upper(), upper_own, lower_own)}
    values["token"] = pack([(values["q0"], 0, TILE)])
    up, down = functools.partial(along, shift=1), functools.partial(along, shift=-1)
    flip, over = (functools.partial(plane, hop=both_cores(hop)) for hop in ((1, 0), (0, 1)))
    moves = {
        "p1": (up, "p0"),
        "p2": (down, "p0"),
        "p3": (up, "p1"),
        "l1": (up, "l0"),
        "l2": (down, "l0"),
        "l3": (up, "l1"),
        **{f"a{i}": (a_hop, f"p{i}") for i in range(4)},
        **{f"b{i}": (b_hop, f"p{i}") for i in range(4)},
        "d0": (b_hop, "a0"),
        "d1": (up, "d0") if DIAGONAL["d1"] == "z" else (b_hop, "a1"),
        "d2": (down, "d0") if DIAGONAL["d2"] == "z" else (b_hop, "a2"),
        "d3": (up, "d1") if DIAGONAL["d3"] == "z" else (b_hop, "a3"),
        **{f"t{m}": (sibling, f"m{m}") for m in ("01", "2", "3", "x")},
        "td": (sibling, "d3"),
        "xx": (flip, "x0"),
        "xy": (over, "x1"),
    }

    def packed(*names):
        return names, lambda: pack([values[n] for n in names])

    def extend():
        return call(
            extend_kernel,
            single(rows + TILE, cols),
            [material_ids, transmit_fwd, values["token"]],
            far=(0,),
            loose=(2,),
            scratch=[pltpu.SMEM(material_ids.shape, jnp.int32), pltpu.SemaphoreType.DMA],
        )

    def scale():
        outs = [single(rows, cols), single(-(-order // cols // TILE) * TILE, cols)]
        operands = [values["x0"], values["xx"], interface_gain]
        panel, values["weight"] = call(functools.partial(scale_kernel, grid), outs, operands)
        return panel

    made = {
        "p0": ((), lambda: pack([(values["q0"], 0, rows)])),
        "l0": ((), lambda: pack([(values["q0"], rows, 2 * rows)])),
        "x0": ((), extend),
        "x1": (("xx",), scale),
        "m01": packed("p0", "p1", "a0", "a1", "b0", "b1", "d0", "d1"),
        "m2": packed("p2", "a2", "b2", "d2"),
        "m3": packed("p3", "a3", "b3"),
        "mx": packed("x1", "xy"),
    }
    kernels = {"01": (2, 2 * rows), "2": (1, rows)}

    def absorb_named(name):
        new, height = kernels[name]
        absorb([values[f"m{name}"], values[f"t{name}"]], new, height, 1, [])

    def pass_gate(gate_number, *needs):
        starting = [t for t in SLOTS if t in moves and SLOTS[t][0] == gate_number]
        ending = [t for t in SLOTS if t in moves and SLOTS[t][1] == gate_number]
        needs = list(needs)
        for name, number in KERNELS.items():
            if number == gate_number:
                absorb_named(name)
                needs.append(highs[-1])
        passed = ["token"]
        for t in starting:
            source = moves[t][1]
            if source not in values:
                sources = made[source][0]
                source = max(sources, key=lambda n: SLOTS[n][1] if n in SLOTS else -1) if sources else "token"
            if source not in passed:
                passed.append(source)
        needs += [values[t] for t in ending if t not in passed]
        for name, value in zip(passed, gate([values[n] for n in passed], *needs)):
            values[name] = value
        for t in starting:
            function, source = moves[t]
            if source not in values:
                values[source] = made[source][1]()
            with jax.named_scope(t):
                values[t] = function(values[source])

    for gate_number in range(ANCHOR + 1):
        pass_gate(gate_number)
    for name in ("01", "2"):
        if name not in KERNELS:
            absorb_named(name)
    width = cols // cores
    operands = [values[n] for n in ("m3", "d3", "t3", "td")] + [*highs, *lows, *sums, values["mx"], values["tx"]]
    part, high, low = call(
        functools.partial(horner_kernel, grid),
        [single(order, width), half, half],
        [*operands, values["token"]],
        loose=(len(operands),),
        scratch=[pltpu.VMEM((order, order), jnp.bfloat16)] * 2 + [pltpu.VMEM((order, 2 * width), jnp.bfloat16), pltpu.VMEM((order, width), jnp.float32)],
        flops=10 * 6 * NTERMS * order * order * width,
        limit=10 * MIB,
    )
    highs, lows = highs + [high], lows + [low]
    parts = [part] + ([sibling(part)] if cores == 2 else [])
    for gate_number in range(ANCHOR + 1, 1 + max(t[1] for t in SLOTS.values())):
        pass_gate(gate_number, part)
    left = [values[n] for n in ("l0", "l1", "l2", "l3")]
    operands = highs + lows + left + [values["weight"]]
    left = call(
        functools.partial(left_kernel, grid),
        [jax.ShapeDtypeStruct((rows, order), jnp.bfloat16)] * 2,
        [*operands, values["token"]],
        loose=(len(operands),),
        flops=6 * rows * order * order,
    )
    result = call(
        functools.partial(last_kernel, grid),
        single(rows, cols),
        [*left, reflect_fwd, *parts],
        scratch=[pltpu.VMEM((order, cols), jnp.bfloat16)] * 2,
        flops=6 * rows * order * cols,
    )
    across = plane(result, both_cores((1, 0)))
    outs = [single(1, rows, cols)] * 2
    return tuple(call(functools.partial(finish_kernel, grid), outs, [result, across]))


def solution(mesh):
    block = P("layer", "row", "col")
    return jax.shard_map(
        on_device,
        mesh=mesh,
        in_specs=(block, block, block, block, P("layer"), P()),
        out_specs=(block, block),
        check_vma=False,
    )
```

```python
import functools

import jax
import jax.numpy as jnp
from jax import lax
from jax.experimental import pallas as pl
from jax.experimental.pallas import tpu as pltpu
from jax.sharding import PartitionSpec as P

NTERMS = 6
MIB = 2**20
TILE = 8
GATE = 2 * 10**10

SLOTS = {
    "p1": (1, 3),
    "a0": (0, 2),
    "b0": (0, 2),
    "t01": (7, 9),
    "xx": (1, 3),
    "p2": (2, 4),
    "d0": (2, 4),
    "a1": (3, 5),
    "b1": (4, 7),
    "p3": (3, 5),
    "xy": (3, 5),
    "d1": (5, 7),
    "a3": (5, 7),
    "d2": (6, 8),
    "b2": (6, 8),
    "b3": (7, 9),
    "d3": (7, 10),
    "t2": (8, 10),
    "td": (10, 11),
    "l1": (9, 11),
    "t3": (9, 11),
    "tx": (8, 10),
    "a2": (4, 6),
    "l2": (10, 12),
    "l3": (11, 12),
}
KERNELS = {'01': 9, '2': 10}
DIAGONAL = {'d1': 'p', 'd2': 'z', 'd3': 'p'}
ANCHOR = 11


class Grid:
    def __init__(self, shape, layers, row_count, blocks):
        self.shape = shape
        self.layers, self.row_count, self.blocks = layers, row_count, blocks
        self.distance = layers // 2
        self.cores = 2 if row_count % 2 == 0 else 1
        self.chips = row_count // self.cores
        self.hops = [((0, 0), (0, 0))]
        if self.chips == 2:
            self.hops += [((1, 0), (0, 1)), ((0, 1), (1, 0)), ((1, 1), (1, 1))]
        else:
            self.hops += [((1, 0), (1, 0))]
            self.hops += [((f, h), (f, h)) for f in (0, 1) for h in range(1, self.chips)]

    def upper(self):
        return lax.axis_index("layer") < self.distance

    def row(self):
        return lax.axis_index("row")

    def place(self, k):
        hop = k // 2 if k % 2 == 0 else self.blocks - k // 2 - 1
        return lax.rem(lax.axis_index("col") + hop, self.blocks)

    def row_of(self, hop, other):
        row = self.row()
        core = lax.rem(row, self.cores)
        chip = lax.rem(lax.div(row, self.cores) + self.chips - hop, self.chips)
        return chip * self.cores + (self.cores - 1 - core if other else core)

    def origins(self):
        side = jnp.where(self.upper(), 0, 1)
        odd = lax.rem(self.row(), self.cores)
        found = []
        for other in range(self.cores):
            for even_hop, odd_hop in self.hops:
                on_odd = (1 - odd if other else odd) == 1
                flip = jnp.where(on_odd, odd_hop[0], even_hop[0])
                hop = jnp.where(on_odd, odd_hop[1], even_hop[1])
                found.append((jnp.where(flip == 1, 1 - side, side), self.row_of(hop, other)))
        return found


def split(value):
    high = value.astype(jnp.bfloat16)
    return high, (value - high.astype(jnp.float32)).astype(jnp.bfloat16)


def dot(left, right):
    return jnp.dot(left, right, preferred_element_type=jnp.float32)


def dot3(left_high, left_low, right_high, right_low):
    return dot(left_high, right_high) + (dot(left_high, right_low) + dot(left_low, right_high))


def span(index, size):
    return pl.ds(pl.multiple_of(index * size, size), size)


def extend_kernel(ids, block, late, out, number, sem):
    del late
    rows = block.shape[1]
    copy = pltpu.make_async_copy(ids, number, sem)
    copy.start()
    out[:rows, :] = block[0]
    copy.wait()
    out[rows:, :] = jnp.full((TILE, out.shape[1]), number[0].astype(jnp.float32))


def scale_kernel(grid, own, across, gains, panel, weight):
    rows, cols = grid.shape

    def gain(block, i):
        number = block[rows : rows + 1, :]
        here = pl.ds(i * cols, cols)
        return sum(jnp.where(number == m, gains[m : m + 1, here], 0.0) for m in range(gains.shape[0]))

    for i in range(gains.shape[1] // cols):
        weight[i : i + 1, :] = gain(own, i) * gain(across, i)
    here = weight[pl.ds(lax.div(grid.row() * rows, cols), 1), :]
    column = jnp.concatenate([here] * 8, axis=0).T[:, :1]
    panel[...] = jnp.where(grid.upper(), own[:rows, :], across[:rows, :]) * column


def gate_kernel(count, *refs):
    for value, out in zip(refs[:count], refs[-count:]):
        out[...] = value[...]


def pack_kernel(parts, *refs):
    here = 0
    for ref, (start, stop) in zip(refs, parts):
        refs[-1][here : here + stop - start, :] = ref[start:stop, :]
        here += stop - start


def ingest(grid, refs, new, height, highs, lows):
    rows = grid.shape[0]
    pieces = [ref.at[pl.ds(i, height), :] for ref in refs for i in range(0, ref.shape[0], height)]
    for piece, (side, row) in zip(pieces, grid.origins()):
        for j in range(new):
            high, low = split(piece[j * rows : (j + 1) * rows, :])
            highs[j][side, span(row, rows), :] = high
            lows[j][side, span(row, rows), :] = low


def absorb_kernel(grid, done, new, height, mine, theirs, *refs):
    cols = grid.shape[1]
    old, sums = refs[: 2 * done], refs[2 * done : 3 * done]
    refs = refs[-(3 * new + done) :]
    fresh, out_sums = refs[: 2 * new], refs[2 * new :]
    highs, lows = old[:done] + fresh[:new], old[done:] + fresh[new:]
    ingest(grid, [mine, theirs], new, height, fresh[:new], fresh[new:])
    for n in range(done + new):
        total = sums[n][...] if n < done else None
        for k in range(done if n < done else 0, done + new):
            here = span(grid.place(k), cols)
            term = dot3(highs[k][0], lows[k][0], highs[n][1, here, :], lows[n][1, here, :])
            total = term if total is None else total + term
        out_sums[n][...] = total


def horner_kernel(grid, *refs):
    rows, cols = grid.shape
    blocks = grid.blocks
    old = blocks - 1
    last, refs = refs[:4], refs[4:]
    highs, lows, sums, refs = refs[:old], refs[old : 2 * old], refs[2 * old : 3 * old], refs[3 * old :]
    mine_x, theirs_x, _, out, high, low, power_high, power_low, pair, base = refs
    width = out.shape[1]
    ingest(grid, last, 1, rows, [high], [low])
    highs, lows = (*highs, high), (*lows, low)
    places = [grid.place(j) for j in range(blocks)]
    for n in range(blocks):
        total = sums[n][...] if n < old else None
        for k in range(old if n < old else 0, blocks):
            here = span(places[k], cols)
            term = dot3(highs[k][0], lows[k][0], highs[n][1, here, :], lows[n][1, here, :])
            total = term if total is None else total + term
        here = pl.ds(n * cols, cols)
        power_high[:, here], power_low[:, here] = split(total)

    ours = span(lax.rem(grid.row(), grid.cores), width)

    def take(read):
        for j in range(blocks):
            z_high, z_low = split(read(span(places[j], cols)))
            here = pl.ds(j * cols, cols)
            pair[here, :width], pair[here, width:] = z_high, z_low

    pieces = [ref.at[pl.ds(i, rows), :] for ref in (mine_x, theirs_x) for i in range(0, ref.shape[0], rows)]
    starts = [grid.row_of(hop, other) for other in range(grid.cores) for hop in range(grid.chips)]
    for piece, start in zip(pieces, starts):
        base[span(start, rows), :] = piece[:, ours]
    take(lambda here: base[here, :])

    @pl.loop(0, NTERMS - 1)
    def _(_):
        both = dot(power_high[...], pair[...])
        rest = dot(power_low[...], pair[:, :width])
        out[...] = base[...] + (both[:, :width] + (both[:, width:] + rest))
        take(lambda here: out[here, :])


def part_kernel(grid, count, *refs):
    blocks = grid.blocks
    highs, lows, left, (weight, out) = refs[:blocks], refs[blocks : 2 * blocks], refs[2 * blocks : 2 * blocks + count], refs[-2:]
    cols = grid.shape[1]

    @pl.when(grid.upper())
    def _():
        places = [grid.place(j) for j in range(count)]
        scaled = [split(left[j][...] * weight[pl.ds(places[j], 1), :]) for j in range(count)]
        for n in range(blocks):
            total = None
            for j in range(count):
                term = dot3(*scaled[j], highs[n][1, span(places[j], cols), :], lows[n][1, span(places[j], cols), :])
                total = term if total is None else total + term
            out[:, n * cols : (n + 1) * cols] = total


def left_kernel(grid, *refs):
    blocks = grid.blocks
    highs, lows, left, refs = refs[:blocks], refs[blocks : 2 * blocks], refs[2 * blocks : 3 * blocks], refs[3 * blocks :]
    weight, part, _, left_high, left_low = refs
    cols = grid.shape[1]

    @pl.when(grid.upper())
    def _():
        place = grid.place(blocks - 1)
        scaled = split(left[-1][...] * weight[pl.ds(place, 1), :])
        for n in range(blocks):
            here = pl.ds(n * cols, cols)
            term = dot3(*scaled, highs[n][1, span(place, cols), :], lows[n][1, span(place, cols), :])
            left_high[:, here], left_low[:, here] = split(part[:, here] + term)

    @pl.when(jnp.logical_not(grid.upper()))
    def _():
        for n in range(blocks):
            here = pl.ds(n * cols, cols)
            left_high[:, here], left_low[:, here] = split(left[n][...])


def last_kernel(grid, left_high, left_low, reflect, *refs):
    parts, (out, z_high, z_low) = refs[:-3], refs[-3:]
    cols = grid.shape[1]
    width = parts[0].shape[1]
    core = lax.rem(grid.row(), grid.cores)
    for i, part in enumerate(parts):
        ours = span(core if i == 0 else 1 - core, width)
        for j in range(grid.blocks):
            here = pl.ds(j * cols, cols)
            z_high[here, ours], z_low[here, ours] = split(part[span(grid.place(j), cols), :])
    result = dot3(left_high[...], left_low[...], z_high[...], z_low[...])
    out[...] = jnp.where(grid.upper(), reflect[0] + result, result)


def finish_kernel(grid, own, across, reflect, transmit):
    upper = grid.upper()
    reflect[0] = jnp.where(upper, own[...], across[...])
    transmit[0] = jnp.where(upper, across[...], own[...])


def call(kernel, outs, operands, scalars=(), loose=(), far=(), scratch=(), aliases=None, flops=0, moved=0, limit=4 * MIB):
    spaces = [pltpu.VMEM] * len(operands)
    for numbers, space in ((scalars, pltpu.SMEM), (far, pltpu.HBM), (loose, pl.ANY)):
        for i in numbers:
            spaces[i] = space
    specs = [pl.BlockSpec(memory_space=space) for space in spaces]
    return pl.pallas_call(
        kernel,
        out_shape=outs,
        in_specs=specs,
        out_specs=jax.tree.map(lambda _: pl.BlockSpec(memory_space=pltpu.VMEM), outs),
        scratch_shapes=list(scratch),
        input_output_aliases=aliases or {},
        compiler_params=pltpu.CompilerParams(vmem_limit_bytes=limit),
        cost_estimate=pl.CostEstimate(flops=flops, bytes_accessed=moved, transcendentals=0),
    )(*operands)


def single(*shape):
    return jax.ShapeDtypeStruct(shape, jnp.float32)


def gate(values, *needs):
    count = len(values)
    kernel = functools.partial(gate_kernel, count)
    return call(kernel, [single(*v.shape) for v in values], [*values, *needs], loose=range(count, count + len(needs)), flops=GATE, moved=10 * GATE)


def pack(blocks, *needs):
    blocks = [b if isinstance(b, tuple) else (b, 0, b.shape[0]) for b in blocks]
    parts = [b[1:] for b in blocks]
    arrays = [b[0] for b in blocks]
    shape = (sum(stop - start for start, stop in parts), arrays[0].shape[1])
    loose = range(len(arrays), len(arrays) + len(needs))
    return call(functools.partial(pack_kernel, parts), single(*shape), [*arrays, *needs], loose=loose)


def on_device(reflect_fwd, transmit_fwd, reflect_bwd, transmit_bwd, material_ids, interface_gain):
    rows, cols = reflect_fwd.shape[1:]
    grid = Grid((rows, cols), *(lax.axis_size(a) for a in ("layer", "row", "col")))
    blocks, hops, cores, chips = grid.blocks, grid.hops, grid.cores, grid.chips
    order = rows * grid.row_count

    def plane(value, hop):
        route = []
        for layer in range(grid.layers):
            for row in range(grid.row_count):
                flip, on = hop[row % cores]
                target = (layer + grid.distance) % grid.layers if flip else layer
                route.append((layer * grid.row_count + row, target * grid.row_count + (row + on * cores) % grid.row_count))
        return lax.ppermute(value, ("layer", "row"), route)

    def both_cores(hop):
        return (hop, hop)

    def sibling(value):
        return lax.ppermute(value, "row", [(i, i ^ 1) for i in range(grid.row_count)])

    def ring(found, top=None):
        k = len(found)
        source = found[max(k - 2, 0)] if top is None else top
        shift = 1 if k % 2 else -1
        found.append(lax.ppermute(source, "col", [(i, (i + shift) % blocks) for i in range(blocks)]))

    highs, lows, sums = [], [], []
    half = jax.ShapeDtypeStruct((2, order, cols), jnp.bfloat16)

    def absorb(pieces, new, height, weight, needs):
        nonlocal highs, lows, sums
        done = len(highs)
        operands = pieces + highs + lows + sums
        results = call(
            functools.partial(absorb_kernel, grid, done, new, height),
            [half] * (2 * new) + [single(order, cols)] * (done + new),
            operands + list(needs),
            loose=range(len(operands), len(operands) + len(needs)),
            aliases={len(operands) - done + n: 2 * new + n for n in range(done)},
            flops=int(weight * 6 * new * (2 * done + new) * order * cols * cols),
        )
        results = list(results)
        highs, lows, sums = highs + results[:new], lows + results[new : 2 * new], results[2 * new :]

    def along(value, shift):
        return lax.ppermute(value, "col", [(i, (i + shift) % blocks) for i in range(blocks)])

    def a_hop(value):
        return plane(value, hops[1])

    def b_hop(value):
        return plane(value, hops[2])

    upper_own = jnp.concatenate([reflect_bwd[0], transmit_bwd[0]], axis=0)
    lower_own = jnp.concatenate([reflect_fwd[0], transmit_fwd[0]], axis=0)
    values = {"q0": jnp.where(grid.upper(), upper_own, lower_own)}
    values["token"] = pack([(values["q0"], 0, TILE)])
    up, down = functools.partial(along, shift=1), functools.partial(along, shift=-1)
    flip, over = (functools.partial(plane, hop=both_cores(hop)) for hop in ((1, 0), (0, 1)))
    moves = {
        "p1": (up, "p0"),
        "p2": (down, "p0"),
        "p3": (up, "p1"),
        "l1": (up, "l0"),
        "l2": (down, "l0"),
        "l3": (up, "l1"),
        **{f"a{i}": (a_hop, f"p{i}") for i in range(4)},
        **{f"b{i}": (b_hop, f"p{i}") for i in range(4)},
        "d0": (b_hop, "a0"),
        "d1": (up, "d0") if DIAGONAL["d1"] == "z" else (b_hop, "a1"),
        "d2": (down, "d0") if DIAGONAL["d2"] == "z" else (b_hop, "a2"),
        "d3": (up, "d1") if DIAGONAL["d3"] == "z" else (b_hop, "a3"),
        **{f"t{m}": (sibling, f"m{m}") for m in ("01", "2", "3", "x")},
        "td": (sibling, "d3"),
        "xx": (flip, "x0"),
        "xy": (over, "x1"),
    }

    def packed(*names):
        return names, lambda: pack([values[n] for n in names])

    def extend():
        return call(
            extend_kernel,
            single(rows + TILE, cols),
            [material_ids, transmit_fwd, values["token"]],
            far=(0,),
            loose=(2,),
            scratch=[pltpu.SMEM(material_ids.shape, jnp.int32), pltpu.SemaphoreType.DMA],
        )

    def scale():
        outs = [single(rows, cols), single(-(-order // cols // TILE) * TILE, cols)]
        operands = [values["x0"], values["xx"], interface_gain]
        panel, values["weight"] = call(functools.partial(scale_kernel, grid), outs, operands)
        return panel

    made = {
        "p0": ((), lambda: pack([(values["q0"], 0, rows)])),
        "l0": ((), lambda: pack([(values["q0"], rows, 2 * rows)])),
        "x0": ((), extend),
        "x1": (("xx",), scale),
        "m01": packed("p0", "p1", "a0", "a1", "b0", "b1", "d0", "d1"),
        "m2": packed("p2", "a2", "b2", "d2"),
        "m3": packed("p3", "a3", "b3"),
        "mx": packed("x1", "xy"),
    }
    kernels = {"01": (2, 2 * rows), "2": (1, rows)}

    def absorb_named(name):
        new, height = kernels[name]
        absorb([values[f"m{name}"], values[f"t{name}"]], new, height, 1, [])

    def pass_gate(gate_number, *needs):
        starting = [t for t in SLOTS if t in moves and SLOTS[t][0] == gate_number]
        ending = [t for t in SLOTS if t in moves and SLOTS[t][1] == gate_number]
        needs = list(needs)
        for name, number in KERNELS.items():
            if number == gate_number:
                absorb_named(name)
                needs.append(highs[-1])
        passed = ["token"]
        for t in starting:
            source = moves[t][1]
            if source not in values:
                sources = made[source][0]
                source = max(sources, key=lambda n: SLOTS[n][1] if n in SLOTS else -1) if sources else "token"
            if source not in passed:
                passed.append(source)
        needs += [values[t] for t in ending if t not in passed]
        for name, value in zip(passed, gate([values[n] for n in passed], *needs)):
            values[name] = value
        for t in starting:
            function, source = moves[t]
            if source not in values:
                values[source] = made[source][1]()
            with jax.named_scope(t):
                values[t] = function(values[source])

    for gate_number in range(ANCHOR + 1):
        pass_gate(gate_number)
    for name in ("01", "2"):
        if name not in KERNELS:
            absorb_named(name)
    width = cols // cores
    operands = [values[n] for n in ("m3", "d3", "t3", "td")] + [*highs, *lows, *sums, values["mx"], values["tx"]]
    part, high, low = call(
        functools.partial(horner_kernel, grid),
        [single(order, width), half, half],
        [*operands, values["token"]],
        loose=(len(operands),),
        scratch=[pltpu.VMEM((order, order), jnp.bfloat16)] * 2 + [pltpu.VMEM((order, 2 * width), jnp.bfloat16), pltpu.VMEM((order, width), jnp.float32)],
        flops=10 * 6 * NTERMS * order * order * width,
        limit=10 * MIB,
    )
    highs, lows = highs + [high], lows + [low]
    parts = [part] + ([sibling(part)] if cores == 2 else [])
    first = [values[n] for n in ("l0", "l1", "l2")]
    partial = call(
        functools.partial(part_kernel, grid, len(first)),
        single(rows, order),
        highs + lows + first + [values["weight"]],
        flops=6 * rows * order * order,
    )
    for gate_number in range(ANCHOR + 1, 1 + max(t[1] for t in SLOTS.values())):
        pass_gate(gate_number, part, partial)
    left = [values[n] for n in ("l0", "l1", "l2", "l3")]
    operands = highs + lows + left + [values["weight"], partial]
    left = call(
        functools.partial(left_kernel, grid),
        [jax.ShapeDtypeStruct((rows, order), jnp.bfloat16)] * 2,
        [*operands, values["token"]],
        loose=(len(operands),),
        flops=6 * rows * order * order,
    )
    result = call(
        functools.partial(last_kernel, grid),
        single(rows, cols),
        [*left, reflect_fwd, *parts],
        scratch=[pltpu.VMEM((order, cols), jnp.bfloat16)] * 2,
        flops=6 * rows * order * cols,
    )
    across = plane(result, both_cores((1, 0)))
    outs = [single(1, rows, cols)] * 2
    return tuple(call(functools.partial(finish_kernel, grid), outs, [result, across]))


def solution(mesh):
    block = P("layer", "row", "col")
    return jax.shard_map(
        on_device,
        mesh=mesh,
        in_specs=(block, block, block, block, P("layer"), P()),
        out_specs=(block, block),
        check_vma=False,
    )
```

```python
import functools

import jax
import jax.numpy as jnp
from jax import lax
from jax.experimental import pallas as pl
from jax.experimental.pallas import tpu as pltpu
from jax.sharding import PartitionSpec as P

NTERMS = 6
MIB = 2**20
TILE = 8
GATE = 2 * 10**10

SLOTS = {
    "p1": (1, 3),
    "a0": (0, 2),
    "b0": (0, 2),
    "t01": (7, 9),
    "xx": (1, 3),
    "p2": (2, 4),
    "d0": (2, 4),
    "a1": (3, 5),
    "b1": (4, 7),
    "p3": (3, 5),
    "xy": (3, 5),
    "d1": (5, 7),
    "a3": (5, 7),
    "d2": (6, 8),
    "b2": (6, 8),
    "b3": (7, 9),
    "d3": (7, 10),
    "t2": (8, 10),
    "td": (10, 11),
    "l1": (8, 10),
    "t3": (9, 11),
    "tx": (8, 10),
    "a2": (4, 6),
    "l2": (10, 12),
    "l3": (10, 12),
}
KERNELS = {'01': 9, '2': 10}
DIAGONAL = {'d1': 'p', 'd2': 'z', 'd3': 'p'}
ANCHOR = 11


class Grid:
    def __init__(self, shape, layers, row_count, blocks):
        self.shape = shape
        self.layers, self.row_count, self.blocks = layers, row_count, blocks
        self.distance = layers // 2
        self.cores = 2 if row_count % 2 == 0 else 1
        self.chips = row_count // self.cores
        self.hops = [((0, 0), (0, 0))]
        if self.chips == 2:
            self.hops += [((1, 0), (0, 1)), ((0, 1), (1, 0)), ((1, 1), (1, 1))]
        else:
            self.hops += [((1, 0), (1, 0))]
            self.hops += [((f, h), (f, h)) for f in (0, 1) for h in range(1, self.chips)]

    def upper(self):
        return lax.axis_index("layer") < self.distance

    def row(self):
        return lax.axis_index("row")

    def place(self, k):
        hop = k // 2 if k % 2 == 0 else self.blocks - k // 2 - 1
        return lax.rem(lax.axis_index("col") + hop, self.blocks)

    def row_of(self, hop, other):
        row = self.row()
        core = lax.rem(row, self.cores)
        chip = lax.rem(lax.div(row, self.cores) + self.chips - hop, self.chips)
        return chip * self.cores + (self.cores - 1 - core if other else core)

    def origins(self):
        side = jnp.where(self.upper(), 0, 1)
        odd = lax.rem(self.row(), self.cores)
        found = []
        for other in range(self.cores):
            for even_hop, odd_hop in self.hops:
                on_odd = (1 - odd if other else odd) == 1
                flip = jnp.where(on_odd, odd_hop[0], even_hop[0])
                hop = jnp.where(on_odd, odd_hop[1], even_hop[1])
                found.append((jnp.where(flip == 1, 1 - side, side), self.row_of(hop, other)))
        return found


def split(value):
    high = value.astype(jnp.bfloat16)
    return high, (value - high.astype(jnp.float32)).astype(jnp.bfloat16)


def dot(left, right):
    return jnp.dot(left, right, preferred_element_type=jnp.float32)


def dot3(left_high, left_low, right_high, right_low):
    return dot(left_high, right_high) + (dot(left_high, right_low) + dot(left_low, right_high))


def span(index, size):
    return pl.ds(pl.multiple_of(index * size, size), size)


def extend_kernel(ids, block, late, out, number, sem):
    del late
    rows = block.shape[1]
    copy = pltpu.make_async_copy(ids, number, sem)
    copy.start()
    out[:rows, :] = block[0]
    copy.wait()
    out[rows:, :] = jnp.full((TILE, out.shape[1]), number[0].astype(jnp.float32))


def scale_kernel(grid, own, across, gains, panel, weight):
    rows, cols = grid.shape

    def gain(block, i):
        number = block[rows : rows + 1, :]
        here = pl.ds(i * cols, cols)
        return sum(jnp.where(number == m, gains[m : m + 1, here], 0.0) for m in range(gains.shape[0]))

    for i in range(gains.shape[1] // cols):
        weight[i : i + 1, :] = gain(own, i) * gain(across, i)
    here = weight[pl.ds(lax.div(grid.row() * rows, cols), 1), :]
    column = jnp.concatenate([here] * 8, axis=0).T[:, :1]
    panel[...] = jnp.where(grid.upper(), own[:rows, :], across[:rows, :]) * column


def gate_kernel(count, *refs):
    for value, out in zip(refs[:count], refs[-count:]):
        out[...] = value[...]


def pack_kernel(parts, *refs):
    here = 0
    for ref, (start, stop) in zip(refs, parts):
        refs[-1][here : here + stop - start, :] = ref[start:stop, :]
        here += stop - start


def ingest(grid, refs, new, height, highs, lows):
    rows = grid.shape[0]
    pieces = [ref.at[pl.ds(i, height), :] for ref in refs for i in range(0, ref.shape[0], height)]
    for piece, (side, row) in zip(pieces, grid.origins()):
        for j in range(new):
            high, low = split(piece[j * rows : (j + 1) * rows, :])
            highs[j][side, span(row, rows), :] = high
            lows[j][side, span(row, rows), :] = low


def absorb_kernel(grid, done, new, height, mine, theirs, *refs):
    cols = grid.shape[1]
    old, sums = refs[: 2 * done], refs[2 * done : 3 * done]
    refs = refs[-(3 * new + done) :]
    fresh, out_sums = refs[: 2 * new], refs[2 * new :]
    highs, lows = old[:done] + fresh[:new], old[done:] + fresh[new:]
    ingest(grid, [mine, theirs], new, height, fresh[:new], fresh[new:])
    for n in range(done + new):
        total = sums[n][...] if n < done else None
        for k in range(done if n < done else 0, done + new):
            here = span(grid.place(k), cols)
            term = dot3(highs[k][0], lows[k][0], highs[n][1, here, :], lows[n][1, here, :])
            total = term if total is None else total + term
        out_sums[n][...] = total


def horner_kernel(grid, *refs):
    rows, cols = grid.shape
    blocks = grid.blocks
    old = blocks - 1
    last, refs = refs[:4], refs[4:]
    highs, lows, sums, refs = refs[:old], refs[old : 2 * old], refs[2 * old : 3 * old], refs[3 * old :]
    mine_x, theirs_x, _, out, high, low, power_high, power_low, pair, base = refs
    width = out.shape[1]
    ingest(grid, last, 1, rows, [high], [low])
    highs, lows = (*highs, high), (*lows, low)
    places = [grid.place(j) for j in range(blocks)]
    for n in range(blocks):
        total = sums[n][...] if n < old else None
        for k in range(old if n < old else 0, blocks):
            here = span(places[k], cols)
            term = dot3(highs[k][0], lows[k][0], highs[n][1, here, :], lows[n][1, here, :])
            total = term if total is None else total + term
        here = pl.ds(n * cols, cols)
        power_high[:, here], power_low[:, here] = split(total)

    ours = span(lax.rem(grid.row(), grid.cores), width)

    def take(read):
        for j in range(blocks):
            z_high, z_low = split(read(span(places[j], cols)))
            here = pl.ds(j * cols, cols)
            pair[here, :width], pair[here, width:] = z_high, z_low

    pieces = [ref.at[pl.ds(i, rows), :] for ref in (mine_x, theirs_x) for i in range(0, ref.shape[0], rows)]
    starts = [grid.row_of(hop, other) for other in range(grid.cores) for hop in range(grid.chips)]
    for piece, start in zip(pieces, starts):
        base[span(start, rows), :] = piece[:, ours]
    take(lambda here: base[here, :])

    @pl.loop(0, NTERMS - 1)
    def _(_):
        both = dot(power_high[...], pair[...])
        rest = dot(power_low[...], pair[:, :width])
        out[...] = base[...] + (both[:, :width] + (both[:, width:] + rest))
        take(lambda here: out[here, :])


def part_kernel(grid, count, *refs):
    blocks = grid.blocks
    highs, lows, left, (weight, out) = refs[:blocks], refs[blocks : 2 * blocks], refs[2 * blocks : 2 * blocks + count], refs[-2:]
    cols = grid.shape[1]

    @pl.when(grid.upper())
    def _():
        places = [grid.place(j) for j in range(count)]
        scaled = [split(left[j][...] * weight[pl.ds(places[j], 1), :]) for j in range(count)]
        for n in range(blocks):
            total = None
            for j in range(count):
                term = dot3(*scaled[j], highs[n][1, span(places[j], cols), :], lows[n][1, span(places[j], cols), :])
                total = term if total is None else total + term
            out[:, n * cols : (n + 1) * cols] = total


def left_kernel(grid, *refs):
    blocks = grid.blocks
    highs, lows, left, refs = refs[:blocks], refs[blocks : 2 * blocks], refs[2 * blocks : 3 * blocks], refs[3 * blocks :]
    weight, part, _, left_high, left_low = refs
    cols = grid.shape[1]

    @pl.when(grid.upper())
    def _():
        place = grid.place(blocks - 1)
        scaled = split(left[-1][...] * weight[pl.ds(place, 1), :])
        for n in range(blocks):
            here = pl.ds(n * cols, cols)
            term = dot3(*scaled, highs[n][1, span(place, cols), :], lows[n][1, span(place, cols), :])
            left_high[:, here], left_low[:, here] = split(part[:, here] + term)

    @pl.when(jnp.logical_not(grid.upper()))
    def _():
        for n in range(blocks):
            here = pl.ds(n * cols, cols)
            left_high[:, here], left_low[:, here] = split(left[n][...])


def last_kernel(grid, left_high, left_low, reflect, *refs):
    parts, (out, z_high, z_low) = refs[:-3], refs[-3:]
    cols = grid.shape[1]
    width = parts[0].shape[1]
    core = lax.rem(grid.row(), grid.cores)
    for i, part in enumerate(parts):
        ours = span(core if i == 0 else 1 - core, width)
        for j in range(grid.blocks):
            here = pl.ds(j * cols, cols)
            z_high[here, ours], z_low[here, ours] = split(part[span(grid.place(j), cols), :])
    result = dot3(left_high[...], left_low[...], z_high[...], z_low[...])
    out[...] = jnp.where(grid.upper(), reflect[0] + result, result)


def finish_kernel(grid, own, across, reflect, transmit):
    upper = grid.upper()
    reflect[0] = jnp.where(upper, own[...], across[...])
    transmit[0] = jnp.where(upper, across[...], own[...])


def call(kernel, outs, operands, scalars=(), loose=(), far=(), scratch=(), aliases=None, flops=0, moved=0, limit=4 * MIB):
    spaces = [pltpu.VMEM] * len(operands)
    for numbers, space in ((scalars, pltpu.SMEM), (far, pltpu.HBM), (loose, pl.ANY)):
        for i in numbers:
            spaces[i] = space
    specs = [pl.BlockSpec(memory_space=space) for space in spaces]
    return pl.pallas_call(
        kernel,
        out_shape=outs,
        in_specs=specs,
        out_specs=jax.tree.map(lambda _: pl.BlockSpec(memory_space=pltpu.VMEM), outs),
        scratch_shapes=list(scratch),
        input_output_aliases=aliases or {},
        compiler_params=pltpu.CompilerParams(vmem_limit_bytes=limit),
        cost_estimate=pl.CostEstimate(flops=flops, bytes_accessed=moved, transcendentals=0),
    )(*operands)


def single(*shape):
    return jax.ShapeDtypeStruct(shape, jnp.float32)


def gate(values, *needs):
    count = len(values)
    kernel = functools.partial(gate_kernel, count)
    return call(kernel, [single(*v.shape) for v in values], [*values, *needs], loose=range(count, count + len(needs)), flops=GATE, moved=10 * GATE)


def pack(blocks, *needs):
    blocks = [b if isinstance(b, tuple) else (b, 0, b.shape[0]) for b in blocks]
    parts = [b[1:] for b in blocks]
    arrays = [b[0] for b in blocks]
    shape = (sum(stop - start for start, stop in parts), arrays[0].shape[1])
    loose = range(len(arrays), len(arrays) + len(needs))
    return call(functools.partial(pack_kernel, parts), single(*shape), [*arrays, *needs], loose=loose)


def on_device(reflect_fwd, transmit_fwd, reflect_bwd, transmit_bwd, material_ids, interface_gain):
    rows, cols = reflect_fwd.shape[1:]
    grid = Grid((rows, cols), *(lax.axis_size(a) for a in ("layer", "row", "col")))
    blocks, hops, cores, chips = grid.blocks, grid.hops, grid.cores, grid.chips
    order = rows * grid.row_count

    def plane(value, hop):
        route = []
        for layer in range(grid.layers):
            for row in range(grid.row_count):
                flip, on = hop[row % cores]
                target = (layer + grid.distance) % grid.layers if flip else layer
                route.append((layer * grid.row_count + row, target * grid.row_count + (row + on * cores) % grid.row_count))
        return lax.ppermute(value, ("layer", "row"), route)

    def both_cores(hop):
        return (hop, hop)

    def sibling(value):
        return lax.ppermute(value, "row", [(i, i ^ 1) for i in range(grid.row_count)])

    def ring(found, top=None):
        k = len(found)
        source = found[max(k - 2, 0)] if top is None else top
        shift = 1 if k % 2 else -1
        found.append(lax.ppermute(source, "col", [(i, (i + shift) % blocks) for i in range(blocks)]))

    highs, lows, sums = [], [], []
    half = jax.ShapeDtypeStruct((2, order, cols), jnp.bfloat16)

    def absorb(pieces, new, height, weight, needs):
        nonlocal highs, lows, sums
        done = len(highs)
        operands = pieces + highs + lows + sums
        results = call(
            functools.partial(absorb_kernel, grid, done, new, height),
            [half] * (2 * new) + [single(order, cols)] * (done + new),
            operands + list(needs),
            loose=range(len(operands), len(operands) + len(needs)),
            aliases={len(operands) - done + n: 2 * new + n for n in range(done)},
            flops=int(weight * 6 * new * (2 * done + new) * order * cols * cols),
        )
        results = list(results)
        highs, lows, sums = highs + results[:new], lows + results[new : 2 * new], results[2 * new :]

    def along(value, shift):
        return lax.ppermute(value, "col", [(i, (i + shift) % blocks) for i in range(blocks)])

    def a_hop(value):
        return plane(value, hops[1])

    def b_hop(value):
        return plane(value, hops[2])

    upper_own = jnp.concatenate([reflect_bwd[0], transmit_bwd[0]], axis=0)
    lower_own = jnp.concatenate([reflect_fwd[0], transmit_fwd[0]], axis=0)
    values = {"q0": jnp.where(grid.upper(), upper_own, lower_own)}
    values["token"] = pack([(values["q0"], 0, TILE)])
    up, down = functools.partial(along, shift=1), functools.partial(along, shift=-1)
    flip, over = (functools.partial(plane, hop=both_cores(hop)) for hop in ((1, 0), (0, 1)))
    moves = {
        "p1": (up, "p0"),
        "p2": (down, "p0"),
        "p3": (up, "p1"),
        "l1": (up, "l0"),
        "l2": (down, "l0"),
        "l3": (up, "l1"),
        **{f"a{i}": (a_hop, f"p{i}") for i in range(4)},
        **{f"b{i}": (b_hop, f"p{i}") for i in range(4)},
        "d0": (b_hop, "a0"),
        "d1": (up, "d0") if DIAGONAL["d1"] == "z" else (b_hop, "a1"),
        "d2": (down, "d0") if DIAGONAL["d2"] == "z" else (b_hop, "a2"),
        "d3": (up, "d1") if DIAGONAL["d3"] == "z" else (b_hop, "a3"),
        **{f"t{m}": (sibling, f"m{m}") for m in ("01", "2", "3", "x")},
        "td": (sibling, "d3"),
        "xx": (flip, "x0"),
        "xy": (over, "x1"),
    }

    def packed(*names):
        return names, lambda: pack([values[n] for n in names])

    def extend():
        return call(
            extend_kernel,
            single(rows + TILE, cols),
            [material_ids, transmit_fwd, values["token"]],
            far=(0,),
            loose=(2,),
            scratch=[pltpu.SMEM(material_ids.shape, jnp.int32), pltpu.SemaphoreType.DMA],
        )

    def scale():
        outs = [single(rows, cols), single(-(-order // cols // TILE) * TILE, cols)]
        operands = [values["x0"], values["xx"], interface_gain]
        panel, values["weight"] = call(functools.partial(scale_kernel, grid), outs, operands)
        return panel

    made = {
        "p0": ((), lambda: pack([(values["q0"], 0, rows)])),
        "l0": ((), lambda: pack([(values["q0"], rows, 2 * rows)])),
        "x0": ((), extend),
        "x1": (("xx",), scale),
        "m01": packed("p0", "p1", "a0", "a1", "b0", "b1", "d0", "d1"),
        "m2": packed("p2", "a2", "b2", "d2"),
        "m3": packed("p3", "a3", "b3"),
        "mx": packed("x1", "xy"),
    }
    kernels = {"01": (2, 2 * rows), "2": (1, rows)}

    def absorb_named(name):
        new, height = kernels[name]
        absorb([values[f"m{name}"], values[f"t{name}"]], new, height, 1, [])

    def pass_gate(gate_number, *needs):
        starting = [t for t in SLOTS if t in moves and SLOTS[t][0] == gate_number]
        ending = [t for t in SLOTS if t in moves and SLOTS[t][1] == gate_number]
        needs = list(needs)
        for name, number in KERNELS.items():
            if number == gate_number:
                absorb_named(name)
                needs.append(highs[-1])
        passed = ["token"]
        for t in starting:
            source = moves[t][1]
            if source not in values:
                sources = made[source][0]
                source = max(sources, key=lambda n: SLOTS[n][1] if n in SLOTS else -1) if sources else "token"
            if source not in passed:
                passed.append(source)
        needs += [values[t] for t in ending if t not in passed]
        for name, value in zip(passed, gate([values[n] for n in passed], *needs)):
            values[name] = value
        for t in starting:
            function, source = moves[t]
            if source not in values:
                values[source] = made[source][1]()
            with jax.named_scope(t):
                values[t] = function(values[source])

    for gate_number in range(ANCHOR + 1):
        pass_gate(gate_number)
    for name in ("01", "2"):
        if name not in KERNELS:
            absorb_named(name)
    width = cols // cores
    operands = [values[n] for n in ("m3", "d3", "t3", "td")] + [*highs, *lows, *sums, values["mx"], values["tx"]]
    part, high, low = call(
        functools.partial(horner_kernel, grid),
        [single(order, width), half, half],
        [*operands, values["token"]],
        loose=(len(operands),),
        scratch=[pltpu.VMEM((order, order), jnp.bfloat16)] * 2 + [pltpu.VMEM((order, 2 * width), jnp.bfloat16), pltpu.VMEM((order, width), jnp.float32)],
        flops=10 * 6 * NTERMS * order * order * width,
        limit=10 * MIB,
    )
    highs, lows = highs + [high], lows + [low]
    parts = [part] + ([sibling(part)] if cores == 2 else [])
    first = [values[n] for n in ("l0", "l1", "l2")]
    partial = call(
        functools.partial(part_kernel, grid, len(first)),
        single(rows, order),
        highs + lows + first + [values["weight"]],
        flops=6 * rows * order * order,
    )
    for gate_number in range(ANCHOR + 1, 1 + max(t[1] for t in SLOTS.values())):
        pass_gate(gate_number, part, partial)
    left = [values[n] for n in ("l0", "l1", "l2", "l3")]
    operands = highs + lows + left + [values["weight"], partial]
    left = call(
        functools.partial(left_kernel, grid),
        [jax.ShapeDtypeStruct((rows, order), jnp.bfloat16)] * 2,
        [*operands, values["token"]],
        loose=(len(operands),),
        flops=6 * rows * order * order,
    )
    result = call(
        functools.partial(last_kernel, grid),
        single(rows, cols),
        [*left, reflect_fwd, *parts],
        scratch=[pltpu.VMEM((order, cols), jnp.bfloat16)] * 2,
        flops=6 * rows * order * cols,
    )
    across = plane(result, both_cores((1, 0)))
    outs = [single(1, rows, cols)] * 2
    return tuple(call(functools.partial(finish_kernel, grid), outs, [result, across]))


def solution(mesh):
    block = P("layer", "row", "col")
    return jax.shard_map(
        on_device,
        mesh=mesh,
        in_specs=(block, block, block, block, P("layer"), P()),
        out_specs=(block, block),
        check_vma=False,
    )
```
